32 devices in a mesh: row: 16 (over z, x, core), col: 2 (over y).
Axes of the slice: x: 2, y: 2, z: 4, core: 2. Of those that a mesh axis runs over, the one named last changes fastest.
Arguments:
- right_sides: float32 [4, 64, 2048], P(None, 'col', 'row'), may hold values from -6 to 6
- factors: bfloat16 [6, 2048, 2048], P(None, 'row', 'col'), may hold values from -0.09375 to 0.09375
- pattern: int32 [6, 16, 16], P(None, 'row', 'col'), may hold values 0 or 1
- live_widths: int32 [4, 16], P(None, 'row'), may hold values from 64 to 128
- inverses: float32 [4, 16, 128, 128], P(None, 'row'), may hold values from -1 to 2, as said below
Outputs:
- solution: float32 [4, 64, 2048], P(None, 'col', 'row')
The draws below stay inside these ranges and needn't reach their ends.
Inputs may be any that keep to these rules, and one draw needn't show every extreme that they name: Each 128 x 128 block of inverses is lower triangular with positive diagonal entries.
All inputs are finite; a program needn't handle non-finite values. No bound on the sum of `pattern` on one device may be relied on, other than what follows from the above.
Results may differ from the reference program's by a relative error of at most 0.0025.
Values may be sent and summed in bfloat16 or wider, within the bound.
No kernel may reach another device: no remote copies, remote signals or barrier semaphores. Data moves between devices by JAX's collectives and lax.ppermute only.
A program may use at most 64 MiB of HBM per device.

```python
import math
import jax
import jax.numpy as jnp
from jax import lax

W = 128
R = 64
LEVELS = 4
K = 16
COLS = 2048
PAIRS = 6


def draw_inverses(key, part):
    diag_key, off_key = jax.random.split(key)
    row_index = jnp.arange(W)[:, None]
    col_index = jnp.arange(W)[None, :]
    below_mask = (col_index < row_index).astype(jnp.float32)
    on_mask = (col_index == row_index).astype(jnp.float32)
    diagonal = jax.random.uniform(diag_key, (LEVELS, K, W), jnp.float32, 0.6, 1.6)
    spread = jnp.clip(jax.random.normal(off_key, (LEVELS, K, W, W), jnp.float32), -4.0, 4.0) * 0.7
    scaled = spread / math.sqrt(W)
    return scaled * below_mask + diagonal[..., None] * on_mask


def with_ends(drawn, rng, smallest, high):
    longest = drawn.shape.index(max(drawn.shape))
    spots = []
    for shift in (0, 1):
        where = [jax.random.randint(jax.random.fold_in(rng, axis), (), 0, length) for axis, length in enumerate(drawn.shape)]
        where[longest] = (where[longest] + shift) % drawn.shape[longest]
        spots.append(tuple(where))
    return drawn.at[spots[0]].set(smallest).at[spots[1]].set(high)


def block_levels(rng, extent, cuts, low, largest):
    loudness = 1.0
    for dim, shards_of in cuts:
        heights = jax.random.uniform(jax.random.fold_in(jax.random.fold_in(rng, 6), dim), (shards_of,), jnp.float32, low / len(cuts), largest / len(cuts))
        loudness = loudness * jnp.repeat(jnp.exp(heights), extent[dim] // shards_of).reshape((-1,) + (1,) * (len(extent) - 1 - dim))
    return loudness


def gaussian(key, extent, scale, limit, cuts=(), kind=jnp.bfloat16):
    array = jax.random.normal(key, extent, jnp.float32) * scale
    if len(cuts) > 0:
        array = block_levels(key, extent, cuts, -0.22, 0.18) * array
    return jnp.clip(array, min=-limit, max=limit).astype(kind)


def setup_inputs(seed: int = 0) -> dict:
    key_of = jax.random.split(jax.random.key(seed), 6)
    return {
        "right_sides": gaussian(key_of[0], (LEVELS, R, COLS), 1.0, 6.0, ((1, 2), (2, 16)), jnp.float32),
        "factors": gaussian(key_of[1], (PAIRS, COLS, COLS), (2 * COLS) ** -0.5, 0.09375, ((1, 16), (2, 2))),
        "pattern": with_ends((jax.random.randint(key_of[2], (PAIRS, K, K), 0, 2) < 1).astype(jnp.int32), jax.random.fold_in(key_of[2], 1), 0, 1),
        "live_widths": with_ends(jax.random.randint(key_of[3], (LEVELS, K), W // 2, W + 1), jax.random.fold_in(key_of[3], 1), W // 2, W).astype(jnp.int32),
        "inverses": draw_inverses(jax.random.fold_in(key_of[5], 71), 0),
    }


def pair_lookup(level_count):
    lookup = {}
    for lower_level in range(level_count):
        for above_level in range(lower_level + 1, level_count):
            lookup[(above_level, lower_level)] = len(lookup)
    return lookup


def live_mask(widths_row, block_width):
    column = jnp.arange(block_width, dtype=jnp.int32)[None, :]
    return (column < widths_row[:, None]).astype(jnp.float32).reshape(-1)


def apply_inverse(vector, inverse, live_part, transpose):
    row_count = vector.shape[0]
    block_count = inverse.shape[0]
    block_width = inverse.shape[1]
    shaped = (vector * live_part).reshape(row_count, block_count, block_width)
    einsum_form = "rkb,kba->rka" if transpose else "rkb,kab->rka"
    result = jnp.einsum(einsum_form, shaped, inverse, precision=lax.Precision.HIGHEST)
    return result.reshape(row_count, block_count * block_width) * live_part


def masked_factor(factor, pattern_pair):
    order_total = factor.shape[0]
    block_count = pattern_pair.shape[0]
    shaped = factor.reshape(block_count, W, block_count, W)
    scaled = shaped * pattern_pair[:, None, :, None].astype(factor.dtype)
    return scaled.reshape(order_total, order_total)


def reference(right_sides, factors, pattern, live_widths, inverses):
    lookup = pair_lookup(LEVELS)
    masks = [live_mask(live_widths[height], W) for height in range(LEVELS)]
    solved = []
    rounded = []
    for height in range(LEVELS):
        accumulated = jnp.zeros((R, COLS), jnp.float32)
        for lower_level in range(height):
            number = lookup[(height, lower_level)]
            matrix = masked_factor(factors[number], pattern[number])
            accumulated = accumulated + jnp.dot(rounded[lower_level], matrix.T, preferred_element_type=jnp.float32)
        current = apply_inverse(right_sides[height] - accumulated, inverses[height], masks[height], False)
        solved.append(current)
        rounded.append(current.astype(jnp.bfloat16))
    results = [None] * LEVELS
    rounded_back = [None] * LEVELS
    for height in reversed(range(LEVELS)):
        accumulated = jnp.zeros((R, COLS), jnp.float32)
        for above_level in range(height + 1, LEVELS):
            number = lookup[(above_level, height)]
            matrix = masked_factor(factors[number], pattern[number])
            accumulated = accumulated + jnp.dot(rounded_back[above_level], matrix, preferred_element_type=jnp.float32)
        current = apply_inverse(solved[height] - accumulated, inverses[height], masks[height], True)
        results[height] = current
        rounded_back[height] = current.astype(jnp.bfloat16)
    return jnp.stack(results)
```

```python
import jax
import jax.numpy as jnp
from jax import lax
from jax.experimental import pallas as pl
from jax.experimental.pallas import tpu as pltpu
from jax.sharding import PartitionSpec as P

HIGHEST = lax.Precision.HIGHEST


def pair_lookup(level_count):
    lookup = {}
    for lower_level in range(level_count):
        for above_level in range(lower_level + 1, level_count):
            lookup[above_level, lower_level] = len(lookup)
    return lookup


def call(kernel, outs, *operands):
    return pl.pallas_call(
        kernel,
        out_shape=outs,
        in_specs=[
            pl.BlockSpec(memory_space=pltpu.SMEM if x.ndim == 1 else pltpu.VMEM) for x in operands
        ],
        out_specs=jax.tree.map(lambda _: pl.BlockSpec(memory_space=pltpu.VMEM), outs),
        compiler_params=pltpu.CompilerParams(vmem_limit_bytes=48 * 1024 * 1024),
    )(*operands)


def live_row(widths, level, block_width):
    column = lax.broadcasted_iota(jnp.int32, (1, block_width), 1)
    return (column < widths[level]).astype(jnp.float32)


def join(blocks):
    return jnp.concatenate([blocks[k] for k in range(blocks.shape[0])], axis=1)


def local(parts, right_sides, factors, pattern, live_widths, inverses):
    row_parts, col_parts = parts
    levels, rhs, width = right_sides.shape
    pairs, _, local_cols = factors.shape
    half = local_cols // width
    total_blocks = half * col_parts
    lookup = pair_lookup(levels)
    widths = live_widths.reshape(levels)
    inverses = inverses.reshape(levels, width, width)
    f32, bf16 = jnp.float32, jnp.bfloat16

    with jax.named_scope("mask"):
        kept = pattern.reshape(pairs, 1, half, 1).astype(bf16)
        masked = (factors.reshape(pairs, width, half, width) * kept).reshape(factors.shape)
    held = {}
    for level in range(1, levels):
        with jax.named_scope("exchange"):
            own = jnp.stack([masked[lookup[level, lower]] for lower in range(level)])
            shifted = [own]
            for shift in range(1, col_parts):
                to_lower = [((q + shift) % col_parts, q) for q in range(col_parts)]
                shifted.append(lax.ppermute(own, "col", to_lower))
            held[level] = shifted

    block_f32 = jax.ShapeDtypeStruct((rhs, width), f32)
    block_bf16 = jax.ShapeDtypeStruct((rhs, width), bf16)
    spread_bf16 = jax.ShapeDtypeStruct((total_blocks, rhs, width), bf16)
    spread_f32 = jax.ShapeDtypeStruct((total_blocks, rhs, width), f32)

    def trade(blocks):
        return lax.all_to_all(blocks, "row", 0, 0)

    def solve_forward(level, widths_ref, rhs_ref, inverse_ref, total):
        live = live_row(widths_ref, level, width)
        vector = (rhs_ref[level] - total) * live
        product = lax.dot_general(
            vector, inverse_ref[level], (((1,), (1,)), ((), ())), precision=HIGHEST, preferred_element_type=f32
        )
        return product * live

    def solve_backward(level, widths_ref, inverse_ref, corrected):
        live = live_row(widths_ref, level, width)
        product = lax.dot_general(
            corrected * live, inverse_ref[level], (((1,), (0,)), ((), ())), precision=HIGHEST, preferred_element_type=f32
        )
        return product * live

    def forward_total(gathered, level, matrices):
        mine = lax.axis_index("col")
        total = None
        for shift in range(col_parts):
            start = lax.rem(mine + shift, col_parts) * half
            for lower in range(level):
                left = join(gathered[lower][pl.ds(start, half)])
                term = lax.dot_general(
                    left, matrices[shift][lower], (((1,), (1,)), ((), ())), preferred_element_type=f32
                )
                total = term if total is None else total + term
        return total

    def backward_partials(out_ref, solved, lower, matrices):
        mine = lax.axis_index("col")
        for shift in range(col_parts):
            start = lax.rem(mine + shift, col_parts) * half
            total = None
            for level, vector in solved.items():
                term = lax.dot_general(
                    vector, matrices[level][shift][lower], (((1,), (0,)), ((), ())), preferred_element_type=f32
                )
                total = term if total is None else total + term
            for block in range(half):
                out_ref[start + block] = total[:, block * width : (block + 1) * width]

    def spread(out_ref, value):
        out_ref[...] = jnp.broadcast_to(value.astype(bf16)[None], out_ref.shape)

    def first(widths_ref, rhs_ref, inverse_ref, solved_ref, out_ref):
        value = solve_forward(0, widths_ref, rhs_ref, inverse_ref, jnp.zeros((rhs, width), f32))
        solved_ref[...] = value
        spread(out_ref, value)

    def middle(level):
        def body(widths_ref, rhs_ref, inverse_ref, *refs):
            gathered, matrices = refs[:level], refs[level : level + col_parts]
            solved_ref, out_ref = refs[level + col_parts :]
            total = forward_total(gathered, level, matrices)
            value = solve_forward(level, widths_ref, rhs_ref, inverse_ref, total)
            solved_ref[...] = value
            spread(out_ref, value)

        return body

    def top(widths_ref, rhs_ref, inverse_ref, *refs):
        level = levels - 1
        gathered, matrices = refs[:level], refs[level : level + col_parts]
        result_ref, rounded_ref, out_ref = refs[level + col_parts :]
        total = forward_total(gathered, level, matrices)
        value = solve_forward(level, widths_ref, rhs_ref, inverse_ref, total)
        result = solve_backward(level, widths_ref, inverse_ref, value)
        result_ref[...] = result
        rounded = result.astype(bf16)
        rounded_ref[...] = rounded
        backward_partials(out_ref, {level: rounded}, level - 1, {level: matrices})

    def down(level):
        above = levels - 1 - level

        def body(widths_ref, inverse_ref, solved_ref, sums_ref, *refs):
            rounded_above = refs[:above]
            flat = refs[above : above + (above + 1) * col_parts]
            result_ref, rounded_ref, out_ref = refs[above + (above + 1) * col_parts :]
            corrected = solved_ref[...] - jnp.sum(sums_ref[...], axis=0)
            result = solve_backward(level, widths_ref, inverse_ref, corrected)
            result_ref[...] = result
            rounded = result.astype(bf16)
            rounded_ref[...] = rounded
            solved = {level: rounded}
            for index in range(above):
                solved[level + 1 + index] = rounded_above[index][...]
            matrices = {
                level + index: flat[index * col_parts : (index + 1) * col_parts] for index in range(above + 1)
            }
            backward_partials(out_ref, solved, level - 1, matrices)

        return body

    def last(widths_ref, inverse_ref, solved_ref, sums_ref, *refs):
        out_ref = refs[-1]
        corrected = solved_ref[...] - jnp.sum(sums_ref[...], axis=0)
        out_ref[0] = solve_backward(0, widths_ref, inverse_ref, corrected)
        for level in range(1, levels):
            out_ref[level] = refs[level - 1][...]

    solved, gathered = [], []
    with jax.named_scope("forward_first"):
        value, out = call(first, (block_f32, spread_bf16), widths, right_sides, inverses)
    solved.append(value)
    gathered.append(trade(out))
    for level in range(1, levels - 1):
        with jax.named_scope("forward_level"):
            value, out = call(
                middle(level), (block_f32, spread_bf16), widths, right_sides, inverses, *gathered, *held[level]
            )
        solved.append(value)
        gathered.append(trade(out))
    results, rounded = {}, {}
    level = levels - 1
    with jax.named_scope("top_level"):
        results[level], rounded[level], out = call(
            top, (block_f32, block_bf16, spread_f32), widths, right_sides, inverses, *gathered, *held[level]
        )
    sums = trade(out)
    for level in range(levels - 2, 0, -1):
        with jax.named_scope("backward_level"):
            flat = [m for upper in range(level, levels) for m in held[upper]]
            results[level], rounded[level], out = call(
                down(level),
                (block_f32, block_bf16, spread_f32),
                widths,
                inverses,
                solved[level],
                sums,
                *[rounded[upper] for upper in range(level + 1, levels)],
                *flat,
            )
        sums = trade(out)
    with jax.named_scope("backward_last"):
        return call(
            last,
            jax.ShapeDtypeStruct((levels, rhs, width), f32),
            widths,
            inverses,
            solved[0],
            sums,
            *[results[level] for level in range(1, levels)],
        )


def solution(mesh):
    parts = (mesh.shape["row"], mesh.shape["col"])

    def run(*operands):
        return local(parts, *operands)

    return jax.shard_map(
        run,
        mesh=mesh,
        in_specs=(
            P(None, "col", "row"),
            P(None, "row", "col"),
            P(None, "row", "col"),
            P(None, "row"),
            P(None, "row", None, None),
        ),
        out_specs=P(None, "col", "row"),
        check_vma=False,
    )
```

```python
import jax
import jax.numpy as jnp
from jax import lax
from jax.experimental import pallas as pl
from jax.experimental.pallas import tpu as pltpu
from jax.sharding import PartitionSpec as P

HIGHEST = lax.Precision.HIGHEST


def pair_lookup(level_count):
    lookup = {}
    for lower_level in range(level_count):
        for above_level in range(lower_level + 1, level_count):
            lookup[above_level, lower_level] = len(lookup)
    return lookup


def call(kernel, outs, *operands, space=pltpu.VMEM, scratch=()):
    return pl.pallas_call(
        kernel,
        out_shape=outs,
        in_specs=[pl.BlockSpec(memory_space=space) for x in operands],
        out_specs=jax.tree.map(lambda _: pl.BlockSpec(memory_space=pltpu.VMEM), outs),
        scratch_shapes=scratch,
        compiler_params=pltpu.CompilerParams(vmem_limit_bytes=48 * 1024 * 1024),
    )(*operands)


def join(blocks):
    return jnp.concatenate([blocks[k] for k in range(blocks.shape[0])], axis=1)


def local(parts, right_sides, factors, pattern, live_widths, inverses):
    row_parts, col_parts = parts
    levels, rhs, width = right_sides.shape
    pairs, _, local_cols = factors.shape
    half = local_cols // width
    total_blocks = half * col_parts
    lookup = pair_lookup(levels)
    needed = [lookup[level, lower] for level in range(1, levels) for lower in range(level)]
    group_size = -(-pairs // (levels - 1))
    groups = [needed[k : k + group_size] for k in range(0, pairs, group_size)]
    place_of = {pair: (g, k) for g, group in enumerate(groups) for k, pair in enumerate(group)}
    inverses = inverses.reshape(levels, width, width)
    f32, bf16 = jnp.float32, jnp.bfloat16

    block_f32 = jax.ShapeDtypeStruct((rhs, width), f32)
    block_bf16 = jax.ShapeDtypeStruct((rhs, width), bf16)
    spread_bf16 = jax.ShapeDtypeStruct((total_blocks, rhs, width), bf16)
    spread_f32 = jax.ShapeDtypeStruct((total_blocks, rhs, width), f32)

    def trade(blocks):
        return lax.all_to_all(blocks, "row", 0, 0)

    def solve_forward(level, live_ref, rhs_ref, inverse_ref, total):
        live = live_ref[level]
        vector = (rhs_ref[level] - total) * live
        product = lax.dot_general(
            vector, inverse_ref[level], (((1,), (1,)), ((), ())), precision=HIGHEST, preferred_element_type=f32
        )
        return product * live

    def solve_backward(level, live_ref, inverse_ref, corrected):
        live = live_ref[level]
        product = lax.dot_general(
            corrected * live, inverse_ref[level], (((1,), (0,)), ((), ())), precision=HIGHEST, preferred_element_type=f32
        )
        return product * live

    def forward_total(gathered, level, matrices):
        mine = lax.axis_index("col")
        total = None
        for shift in range(col_parts):
            start = lax.rem(mine + shift, col_parts) * half
            for lower in range(level):
                left = join(gathered[lower][pl.ds(start, half)])
                term = lax.dot_general(
                    left, matrix(matrices, level, lower, shift), (((1,), (1,)), ((), ())), preferred_element_type=f32
                )
                total = term if total is None else total + term
        return total

    def backward_partials(out_ref, solved, lower, matrices):
        mine = lax.axis_index("col")
        for shift in range(col_parts):
            start = lax.rem(mine + shift, col_parts) * half
            total = None
            for level, vector in solved.items():
                term = lax.dot_general(
                    vector, matrix(matrices, level, lower, shift), (((1,), (0,)), ((), ())), preferred_element_type=f32
                )
                total = term if total is None else total + term
            for block in range(half):
                out_ref[start + block] = total[:, block * width : (block + 1) * width]

    def spread(out_ref, value):
        out_ref[...] = jnp.broadcast_to(value.astype(bf16)[None], out_ref.shape)

    def mask_pair(out_ref, place, pattern_ref, factor_ref, pair):
        for block in range(half):
            columns = slice(block * width, (block + 1) * width)
            kept = jnp.broadcast_to(pattern_ref[pair][:, block : block + 1].astype(f32), (width, width))
            out_ref[place, :, columns] = factor_ref[pair, :, columns] * kept.astype(bf16)

    def first(
        rhs_hbm, factor_hbm, pattern_hbm, widths_hbm, inverse_hbm,
        solved_ref, out_ref, rhs_ref, live_ref, inverse_ref, *refs,
    ):
        masked_refs = refs[: len(groups)]
        factor_ref, pattern_ref, widths_ref, sems = refs[len(groups) :]
        order = needed
        small = [
            pltpu.make_async_copy(pattern_hbm, pattern_ref, sems.at[0]),
            pltpu.make_async_copy(widths_hbm, widths_ref, sems.at[1]),
            pltpu.make_async_copy(rhs_hbm, rhs_ref, sems.at[2]),
            pltpu.make_async_copy(inverse_hbm, inverse_ref, sems.at[3]),
        ]
        large = [
            pltpu.make_async_copy(factor_hbm.at[pair], factor_ref.at[pair], sems.at[4 + k])
            for k, pair in enumerate(order)
        ]
        for copy in small + large:
            copy.start()
        for copy in small:
            copy.wait()
        column = lax.broadcasted_iota(jnp.int32, (1, width), 1)
        for level in range(levels):
            live_ref[level] = (column < widths_ref[level]).astype(f32)
        value = solve_forward(0, live_ref, rhs_ref, inverse_ref, jnp.zeros((rhs, width), f32))
        solved_ref[...] = value
        spread(out_ref, value)
        for copy, pair in zip(large, order):
            copy.wait()
            group, place = place_of[pair]
            mask_pair(masked_refs[group], place, pattern_ref, factor_ref, pair)

    def flat(held):
        return [m for moved in held for m in moved]

    def matrix(refs, level, lower, shift):
        group, place = place_of[lookup[level, lower]]
        return refs[group * col_parts + shift][place]

    def middle(level):
        def body(live_ref, rhs_ref, inverse_ref, *refs):
            gathered, matrices = refs[:level], refs[level:-2]
            solved_ref, out_ref = refs[-2:]
            total = forward_total(gathered, level, matrices)
            value = solve_forward(level, live_ref, rhs_ref, inverse_ref, total)
            solved_ref[...] = value
            spread(out_ref, value)

        return body

    def top(live_ref, rhs_ref, inverse_ref, *refs):
        level = levels - 1
        gathered, matrices = refs[:level], refs[level:-3]
        result_ref, rounded_ref, out_ref = refs[-3:]
        total = forward_total(gathered, level, matrices)
        value = solve_forward(level, live_ref, rhs_ref, inverse_ref, total)
        result = solve_backward(level, live_ref, inverse_ref, value)
        result_ref[...] = result
        rounded = result.astype(bf16)
        rounded_ref[...] = rounded
        backward_partials(out_ref, {level: rounded}, level - 1, matrices)

    def down(level):
        above = levels - 1 - level

        def body(live_ref, inverse_ref, solved_ref, sums_ref, *refs):
            rounded_above = refs[:above]
            matrices = refs[above:-3]
            result_ref, rounded_ref, out_ref = refs[-3:]
            corrected = solved_ref[...] - jnp.sum(sums_ref[...], axis=0)
            result = solve_backward(level, live_ref, inverse_ref, corrected)
            result_ref[...] = result
            rounded = result.astype(bf16)
            rounded_ref[...] = rounded
            solved = {level: rounded}
            for index in range(above):
                solved[level + 1 + index] = rounded_above[index][...]
            backward_partials(out_ref, solved, level - 1, matrices)

        return body

    def last(live_ref, inverse_ref, solved_ref, sums_ref, *refs):
        out_ref = refs[-1]
        corrected = solved_ref[...] - jnp.sum(sums_ref[...], axis=0)
        out_ref[0] = solve_backward(0, live_ref, inverse_ref, corrected)
        for level in range(1, levels):
            out_ref[level] = refs[level - 1][...]

    def exchange(own):
        shifted = [own]
        for shift in range(1, col_parts):
            to_lower = [((q + shift) % col_parts, q) for q in range(col_parts)]
            shifted.append(lax.ppermute(own, "col", to_lower))
        return shifted

    def trade_beside(blocks, group):
        moved = exchange(masked[group]) if group < len(groups) else None
        blocks = trade(blocks)
        for later in range(group + 1, len(groups)):
            masked[later], blocks = lax.optimization_barrier((masked[later], blocks))
        return blocks, moved

    solved, gathered, held = [], [], []
    shaped = lambda *shape: jax.ShapeDtypeStruct(shape, f32)
    with jax.named_scope("forward_first"):
        value, out, right_sides, live, inverses, *masked = call(
            first,
            (block_f32, spread_bf16, shaped(levels, rhs, width), shaped(levels, 1, width), shaped(levels, width, width))
            + tuple(jax.ShapeDtypeStruct((len(group), width, local_cols), bf16) for group in groups),
            right_sides, factors, pattern, live_widths.reshape(levels, 1, 1), inverses,
            space=pltpu.HBM,
            scratch=[
                pltpu.VMEM(factors.shape, bf16),
                pltpu.VMEM(pattern.shape, jnp.int32),
                pltpu.VMEM((levels, 1, 1), jnp.int32),
                pltpu.SemaphoreType.DMA((4 + pairs,)),
            ],
        )
    solved.append(value)
    blocks, moved = trade_beside(out, 0)
    gathered.append(blocks)
    held.append(moved)
    for level in range(1, levels - 1):
        with jax.named_scope("forward_level"):
            value, out = call(middle(level), (block_f32, spread_bf16), live, right_sides, inverses, *gathered, *flat(held))
        solved.append(value)
        blocks, moved = trade_beside(out, level)
        gathered.append(blocks)
        if moved is not None:
            held.append(moved)
    results, rounded = {}, {}
    level = levels - 1
    with jax.named_scope("top_level"):
        results[level], rounded[level], out = call(
            top, (block_f32, block_bf16, spread_f32), live, right_sides, inverses, *gathered, *flat(held)
        )
    sums = trade(out)
    for level in range(levels - 2, 0, -1):
        with jax.named_scope("backward_level"):
            results[level], rounded[level], out = call(
                down(level),
                (block_f32, block_bf16, spread_f32),
                live,
                inverses,
                solved[level],
                sums,
                *[rounded[upper] for upper in range(level + 1, levels)],
                *flat(held),
            )
        sums = trade(out)
    with jax.named_scope("backward_last"):
        return call(
            last,
            jax.ShapeDtypeStruct((levels, rhs, width), f32),
            live,
            inverses,
            solved[0],
            sums,
            *[results[level] for level in range(1, levels)],
        )


def solution(mesh):
    parts = (mesh.shape["row"], mesh.shape["col"])

    def run(*operands):
        return local(parts, *operands)

    return jax.shard_map(
        run,
        mesh=mesh,
        in_specs=(
            P(None, "col", "row"),
            P(None, "row", "col"),
            P(None, "row", "col"),
            P(None, "row"),
            P(None, "row", None, None),
        ),
        out_specs=P(None, "col", "row"),
        check_vma=False,
    )
```

```python
import jax
import jax.numpy as jnp
from jax import lax
from jax.experimental import pallas as pl
from jax.experimental.pallas import tpu as pltpu
from jax.sharding import PartitionSpec as P

HIGHEST = lax.Precision.HIGHEST


def pair_lookup(level_count):
    lookup = {}
    for lower_level in range(level_count):
        for above_level in range(lower_level + 1, level_count):
            lookup[above_level, lower_level] = len(lookup)
    return lookup


def call(kernel, outs, *operands, space=pltpu.VMEM, scratch=()):
    return pl.pallas_call(
        kernel,
        out_shape=outs,
        in_specs=[pl.BlockSpec(memory_space=space) for x in operands],
        out_specs=jax.tree.map(lambda _: pl.BlockSpec(memory_space=pltpu.VMEM), outs),
        scratch_shapes=scratch,
        compiler_params=pltpu.CompilerParams(vmem_limit_bytes=48 * 1024 * 1024),
    )(*operands)


def join(blocks):
    return jnp.concatenate([blocks[k] for k in range(blocks.shape[0])], axis=1)


def local(parts, right_sides, factors, pattern, live_widths, inverses):
    row_parts, col_parts = parts
    levels, rhs, width = right_sides.shape
    pairs, _, local_cols = factors.shape
    half = local_cols // width
    total_blocks = half * col_parts
    lookup = pair_lookup(levels)
    needed = [lookup[level, lower] for level in range(1, levels) for lower in range(level)]
    group_size = -(-pairs // (levels - 1))
    groups = [needed[k : k + group_size] for k in range(0, pairs, group_size)]
    place_of = {pair: (g, k) for g, group in enumerate(groups) for k, pair in enumerate(group)}
    inverses = inverses.reshape(levels, width, width)
    f32, bf16 = jnp.float32, jnp.bfloat16

    block_f32 = jax.ShapeDtypeStruct((rhs, width), f32)
    block_bf16 = jax.ShapeDtypeStruct((rhs, width), bf16)
    spread_bf16 = jax.ShapeDtypeStruct((total_blocks, rhs, width), bf16)
    twins = row_parts // 2
    twins_f32 = jax.ShapeDtypeStruct((twins, rhs, width), f32)

    def trade(blocks):
        return lax.all_to_all(blocks, "row", 0, 0)

    def scatter(keep, give):
        taken = lax.ppermute(give, "row", [(k, k ^ 1) for k in range(row_parts)])
        with jax.named_scope("sum_twins"):
            sums = call(add, twins_f32, keep, taken)
        same_side = [[2 * g + side for g in range(twins)] for side in range(2)]
        return lax.all_to_all(sums, "row", 0, 0, axis_index_groups=same_side)

    def solve_forward(level, live_ref, rhs_ref, inverse_ref, total):
        live = live_ref[level]
        vector = (rhs_ref[level] - total) * live
        product = lax.dot_general(
            vector, inverse_ref[level], (((1,), (1,)), ((), ())), precision=HIGHEST, preferred_element_type=f32
        )
        return product * live

    def solve_backward(level, live_ref, inverse_ref, corrected):
        live = live_ref[level]
        product = lax.dot_general(
            corrected * live, inverse_ref[level], (((1,), (0,)), ((), ())), precision=HIGHEST, preferred_element_type=f32
        )
        return product * live

    def forward_total(gathered, level, matrices):
        mine = lax.axis_index("col")
        total = None
        for shift in range(col_parts):
            start = lax.rem(mine + shift, col_parts) * half
            for lower in range(level):
                left = join(gathered[lower][pl.ds(start, half)])
                term = lax.dot_general(
                    left, matrix(matrices, level, lower, shift), (((1,), (1,)), ((), ())), preferred_element_type=f32
                )
                total = term if total is None else total + term
        return total

    def add(left_ref, right_ref, out_ref):
        out_ref[...] = left_ref[...] + right_ref[...]

    def backward_partials(keep_ref, give_ref, solved, lower, matrices):
        mine = lax.axis_index("col")
        odd = lax.rem(lax.axis_index("row"), 2) == 1
        for shift in range(col_parts):
            start = lax.rem(mine + shift, col_parts) * half
            total = None
            for level, vector in solved.items():
                term = lax.dot_general(
                    vector, matrix(matrices, level, lower, shift), (((1,), (0,)), ((), ())), preferred_element_type=f32
                )
                total = term if total is None else total + term
            for block in range(0, half, 2):
                even = total[:, block * width : (block + 1) * width]
                uneven = total[:, (block + 1) * width : (block + 2) * width]
                keep_ref[start // 2 + block // 2] = jnp.where(odd, uneven, even)
                give_ref[start // 2 + block // 2] = jnp.where(odd, even, uneven)

    def spread(out_ref, value):
        out_ref[...] = jnp.broadcast_to(value.astype(bf16)[None], out_ref.shape)

    def mask_pair(out_ref, place, pattern_ref, factor_ref, pair):
        for block in range(half):
            columns = slice(block * width, (block + 1) * width)
            kept = jnp.broadcast_to(pattern_ref[pair][:, block : block + 1].astype(f32), (width, width))
            out_ref[place, :, columns] = factor_ref[pair, :, columns] * kept.astype(bf16)

    def first(
        rhs_hbm, factor_hbm, pattern_hbm, widths_hbm, inverse_hbm,
        solved_ref, out_ref, rhs_ref, live_ref, inverse_ref, *refs,
    ):
        masked_refs = refs[: len(groups)]
        factor_ref, pattern_ref, widths_ref, sems = refs[len(groups) :]
        order = needed
        small = [
            pltpu.make_async_copy(pattern_hbm, pattern_ref, sems.at[0]),
            pltpu.make_async_copy(widths_hbm, widths_ref, sems.at[1]),
            pltpu.make_async_copy(rhs_hbm, rhs_ref, sems.at[2]),
            pltpu.make_async_copy(inverse_hbm, inverse_ref, sems.at[3]),
        ]
        large = [
            pltpu.make_async_copy(factor_hbm.at[pair], factor_ref.at[pair], sems.at[4 + k])
            for k, pair in enumerate(order)
        ]
        for copy in small + large:
            copy.start()
        for copy in small:
            copy.wait()
        column = lax.broadcasted_iota(jnp.int32, (1, width), 1)
        for level in range(levels):
            live_ref[level] = (column < widths_ref[:, level : level + 1]).astype(f32)
        value = solve_forward(0, live_ref, rhs_ref, inverse_ref, jnp.zeros((rhs, width), f32))
        solved_ref[...] = value
        spread(out_ref, value)
        for copy, pair in zip(large, order):
            copy.wait()
            group, place = place_of[pair]
            mask_pair(masked_refs[group], place, pattern_ref, factor_ref, pair)

    def flat(held):
        return [m for moved in held for m in moved]

    def matrix(refs, level, lower, shift):
        group, place = place_of[lookup[level, lower]]
        return refs[group * col_parts + shift][place]

    def middle(level):
        def body(live_ref, rhs_ref, inverse_ref, *refs):
            gathered, matrices = refs[:level], refs[level:-2]
            solved_ref, out_ref = refs[-2:]
            total = forward_total(gathered, level, matrices)
            value = solve_forward(level, live_ref, rhs_ref, inverse_ref, total)
            solved_ref[...] = value
            spread(out_ref, value)

        return body

    def top(live_ref, rhs_ref, inverse_ref, *refs):
        level = levels - 1
        gathered, matrices = refs[:level], refs[level:-4]
        result_ref, rounded_ref, keep_ref, give_ref = refs[-4:]
        total = forward_total(gathered, level, matrices)
        value = solve_forward(level, live_ref, rhs_ref, inverse_ref, total)
        result = solve_backward(level, live_ref, inverse_ref, value)
        result_ref[...] = result
        rounded = result.astype(bf16)
        rounded_ref[...] = rounded
        backward_partials(keep_ref, give_ref, {level: rounded}, level - 1, matrices)

    def down(level):
        above = levels - 1 - level

        def body(live_ref, inverse_ref, solved_ref, sums_ref, *refs):
            rounded_above = refs[:above]
            matrices = refs[above:-4]
            result_ref, rounded_ref, keep_ref, give_ref = refs[-4:]
            corrected = solved_ref[...] - jnp.sum(sums_ref[...], axis=0)
            result = solve_backward(level, live_ref, inverse_ref, corrected)
            result_ref[...] = result
            rounded = result.astype(bf16)
            rounded_ref[...] = rounded
            solved = {level: rounded}
            for index in range(above):
                solved[level + 1 + index] = rounded_above[index][...]
            backward_partials(keep_ref, give_ref, solved, level - 1, matrices)

        return body

    def last(live_ref, inverse_ref, solved_ref, sums_ref, *refs):
        out_ref = refs[-1]
        corrected = solved_ref[...] - jnp.sum(sums_ref[...], axis=0)
        out_ref[0] = solve_backward(0, live_ref, inverse_ref, corrected)
        for level in range(1, levels):
            out_ref[level] = refs[level - 1][...]

    def exchange(own):
        shifted = [own]
        for shift in range(1, col_parts):
            to_lower = [((q + shift) % col_parts, q) for q in range(col_parts)]
            shifted.append(lax.ppermute(own, "col", to_lower))
        return shifted

    def trade_beside(blocks, group):
        moved = exchange(masked[group]) if group < len(groups) else None
        blocks = trade(blocks)
        for later in range(group + 1, len(groups)):
            masked[later], blocks = lax.optimization_barrier((masked[later], blocks))
        return blocks, moved

    solved, gathered, held = [], [], []
    shaped = lambda *shape: jax.ShapeDtypeStruct(shape, f32)
    with jax.named_scope("forward_first"):
        operands = [
            pltpu.with_memory_space_constraint(x, pltpu.HBM)
            for x in (right_sides, factors, pattern, live_widths.reshape(1, levels), inverses)
        ]
        value, out, right_sides, live, inverses, *masked = call(
            first,
            (block_f32, spread_bf16, shaped(levels, rhs, width), shaped(levels, 1, width), shaped(levels, width, width))
            + tuple(jax.ShapeDtypeStruct((len(group), width, local_cols), bf16) for group in groups),
            *operands,
            space=pltpu.HBM,
            scratch=[
                pltpu.VMEM(factors.shape, bf16),
                pltpu.VMEM(pattern.shape, jnp.int32),
                pltpu.VMEM((1, levels), jnp.int32),
                pltpu.SemaphoreType.DMA((4 + pairs,)),
            ],
        )
    solved.append(value)
    blocks, moved = trade_beside(out, 0)
    gathered.append(blocks)
    held.append(moved)
    for level in range(1, levels - 1):
        with jax.named_scope("forward_level"):
            value, out = call(middle(level), (block_f32, spread_bf16), live, right_sides, inverses, *gathered, *flat(held))
        solved.append(value)
        blocks, moved = trade_beside(out, level)
        gathered.append(blocks)
        if moved is not None:
            held.append(moved)
    results, rounded = {}, {}
    level = levels - 1
    with jax.named_scope("top_level"):
        results[level], rounded[level], *halves = call(
            top, (block_f32, block_bf16, twins_f32, twins_f32), live, right_sides, inverses, *gathered, *flat(held)
        )
    sums = scatter(*halves)
    for level in range(levels - 2, 0, -1):
        with jax.named_scope("backward_level"):
            results[level], rounded[level], *halves = call(
                down(level),
                (block_f32, block_bf16, twins_f32, twins_f32),
                live,
                inverses,
                solved[level],
                sums,
                *[rounded[upper] for upper in range(level + 1, levels)],
                *flat(held),
            )
        sums = scatter(*halves)
    with jax.named_scope("backward_last"):
        return call(
            last,
            jax.ShapeDtypeStruct((levels, rhs, width), f32),
            live,
            inverses,
            solved[0],
            sums,
            *[results[level] for level in range(1, levels)],
        )


def solution(mesh):
    parts = (mesh.shape["row"], mesh.shape["col"])

    def run(*operands):
        return local(parts, *operands)

    return jax.shard_map(
        run,
        mesh=mesh,
        in_specs=(
            P(None, "col", "row"),
            P(None, "row", "col"),
            P(None, "row", "col"),
            P(None, "row"),
            P(None, "row", None, None),
        ),
        out_specs=P(None, "col", "row"),
        check_vma=False,
    )
```

```python
import math

import jax
import jax.numpy as jnp
from jax import lax
from jax.experimental import pallas as pl
from jax.experimental.pallas import tpu as pltpu
from jax.sharding import PartitionSpec as P

HIGHEST = lax.Precision.HIGHEST


def pair_lookup(level_count):
    lookup = {}
    for lower_level in range(level_count):
        for above_level in range(lower_level + 1, level_count):
            lookup[above_level, lower_level] = len(lookup)
    return lookup


def call(kernel, outs, *operands, space=pltpu.VMEM, scratch=()):
    return pl.pallas_call(
        kernel,
        out_shape=outs,
        in_specs=[pl.BlockSpec(memory_space=space) for x in operands],
        out_specs=jax.tree.map(lambda _: pl.BlockSpec(memory_space=pltpu.VMEM), outs),
        scratch_shapes=scratch,
        compiler_params=pltpu.CompilerParams(vmem_limit_bytes=48 * 1024 * 1024),
    )(*operands)


def local(parts, right_sides, factors, pattern, live_widths, inverses):
    row_parts, col_parts = parts
    levels, rhs, width = right_sides.shape
    pairs, _, local_cols = factors.shape
    half = local_cols // width
    total_blocks = half * col_parts
    lookup = pair_lookup(levels)
    needed = [lookup[level, lower] for level in range(1, levels) for lower in range(level)]
    group_size = -(-pairs // (levels - 1))
    groups = [needed[k : k + group_size] for k in range(0, pairs, group_size)]
    place_of = {pair: (g, k) for g, group in enumerate(groups) for k, pair in enumerate(group)}
    inverses = inverses.reshape(levels, width, width)
    f32, bf16 = jnp.float32, jnp.bfloat16

    block_f32 = jax.ShapeDtypeStruct((rhs, width), f32)
    block_bf16 = jax.ShapeDtypeStruct((rhs, width), bf16)
    spread_bf16 = jax.ShapeDtypeStruct((total_blocks, rhs, width), bf16)
    twins = row_parts // 2
    twins_f32 = jax.ShapeDtypeStruct((twins, rhs, width), f32)

    middle_row = row_parts // 2 + 1
    row_order = [middle_row] + [k for k in range(0, row_parts, 2)] + [k for k in range(1, row_parts, 2) if k != middle_row]
    step = next(s for s in range(5, 5 + twins) if math.gcd(s, twins) == 1)
    twin_order = [(twins // 2 + step * k) % twins for k in range(twins)]

    def row_place(index):
        odd_place = twins + index // 2 + jnp.where(index < middle_row, 1, 0)
        odd_place = jnp.where(index == middle_row, 0, odd_place)
        return jnp.where(lax.rem(index, 2) == 0, 1 + index // 2, odd_place)

    def trade(blocks):
        return lax.all_to_all(blocks, "row", 0, 0, axis_index_groups=[row_order])

    def scatter(keep, give):
        taken = lax.ppermute(give, "row", [(k, k ^ 1) for k in range(row_parts)])
        with jax.named_scope("sum_twins"):
            sums = call(add, twins_f32, keep, taken)
        one_of_each = [[2 * g + (g + side) % 2 for g in twin_order] for side in (1, 0)]
        return lax.all_to_all(sums, "row", 0, 0, axis_index_groups=one_of_each)

    def solve_forward(level, live_ref, rhs_ref, inverse_ref, total):
        live = live_ref[level]
        vector = (rhs_ref[level] - total) * live
        product = lax.dot_general(
            vector, inverse_ref[level], (((1,), (1,)), ((), ())), precision=HIGHEST, preferred_element_type=f32
        )
        return product * live

    def solve_backward(level, live_ref, inverse_ref, corrected):
        live = live_ref[level]
        product = lax.dot_general(
            corrected * live, inverse_ref[level], (((1,), (0,)), ((), ())), precision=HIGHEST, preferred_element_type=f32
        )
        return product * live

    def forward_total(gathered, level, matrices):
        mine = lax.axis_index("col")
        total = None
        for shift in range(col_parts):
            start = lax.rem(mine + shift, col_parts) * half
            for lower in range(level):
                left = jnp.concatenate([gathered[lower][row_place(start + k)] for k in range(half)], axis=1)
                term = lax.dot_general(
                    left, matrix(matrices, level, lower, shift), (((1,), (1,)), ((), ())), preferred_element_type=f32
                )
                total = term if total is None else total + term
        return total

    def add(left_ref, right_ref, out_ref):
        for place, g in enumerate(twin_order):
            out_ref[place] = left_ref[g] + right_ref[g]

    def backward_partials(keep_ref, give_ref, solved, lower, matrices):
        mine = lax.axis_index("col")
        index = lax.axis_index("row")
        for shift in range(col_parts):
            start = lax.rem(mine + shift, col_parts) * half
            total = None
            for level, vector in solved.items():
                term = lax.dot_general(
                    vector, matrix(matrices, level, lower, shift), (((1,), (0,)), ((), ())), preferred_element_type=f32
                )
                total = term if total is None else total + term
            for block in range(0, half, 2):
                even = total[:, block * width : (block + 1) * width]
                uneven = total[:, (block + 1) * width : (block + 2) * width]
                g = start // 2 + block // 2
                odd = lax.rem(index + index // 2 + g, 2) == 1
                keep_ref[g] = jnp.where(odd, uneven, even)
                give_ref[g] = jnp.where(odd, even, uneven)

    def spread(out_ref, value):
        out_ref[...] = jnp.broadcast_to(value.astype(bf16)[None], out_ref.shape)

    def mask_pair(out_ref, place, pattern_ref, factor_ref, pair):
        for block in range(half):
            columns = slice(block * width, (block + 1) * width)
            kept = jnp.broadcast_to(pattern_ref[pair][:, block : block + 1].astype(f32), (width, width))
            out_ref[place, :, columns] = factor_ref[pair, :, columns] * kept.astype(bf16)

    def first(
        rhs_hbm, factor_hbm, pattern_hbm, widths_hbm, inverse_hbm,
        solved_ref, out_ref, rhs_ref, live_ref, inverse_ref, *refs,
    ):
        masked_refs = refs[: len(groups)]
        factor_ref, pattern_ref, widths_ref, sems = refs[len(groups) :]
        order = needed
        small = [
            pltpu.make_async_copy(pattern_hbm, pattern_ref, sems.at[0]),
            pltpu.make_async_copy(widths_hbm, widths_ref, sems.at[1]),
            pltpu.make_async_copy(rhs_hbm, rhs_ref, sems.at[2]),
            pltpu.make_async_copy(inverse_hbm, inverse_ref, sems.at[3]),
        ]
        large = [
            pltpu.make_async_copy(factor_hbm.at[pair], factor_ref.at[pair], sems.at[4 + k])
            for k, pair in enumerate(order)
        ]
        for copy in small + large:
            copy.start()
        for copy in small:
            copy.wait()
        column = lax.broadcasted_iota(jnp.int32, (1, width), 1)
        for level in range(levels):
            live_ref[level] = (column < widths_ref[:, level : level + 1]).astype(f32)
        value = solve_forward(0, live_ref, rhs_ref, inverse_ref, jnp.zeros((rhs, width), f32))
        solved_ref[...] = value
        spread(out_ref, value)
        for copy, pair in zip(large, order):
            copy.wait()
            group, place = place_of[pair]
            mask_pair(masked_refs[group], place, pattern_ref, factor_ref, pair)

    def flat(held):
        return [m for moved in held for m in moved]

    def matrix(refs, level, lower, shift):
        group, place = place_of[lookup[level, lower]]
        return refs[group * col_parts + shift][place]

    def middle(level):
        def body(live_ref, rhs_ref, inverse_ref, *refs):
            gathered, matrices = refs[:level], refs[level:-2]
            solved_ref, out_ref = refs[-2:]
            total = forward_total(gathered, level, matrices)
            value = solve_forward(level, live_ref, rhs_ref, inverse_ref, total)
            solved_ref[...] = value
            spread(out_ref, value)

        return body

    def top(live_ref, rhs_ref, inverse_ref, *refs):
        level = levels - 1
        gathered, matrices = refs[:level], refs[level:-4]
        result_ref, rounded_ref, keep_ref, give_ref = refs[-4:]
        total = forward_total(gathered, level, matrices)
        value = solve_forward(level, live_ref, rhs_ref, inverse_ref, total)
        result = solve_backward(level, live_ref, inverse_ref, value)
        result_ref[...] = result
        rounded = result.astype(bf16)
        rounded_ref[...] = rounded
        backward_partials(keep_ref, give_ref, {level: rounded}, level - 1, matrices)

    def down(level):
        above = levels - 1 - level

        def body(live_ref, inverse_ref, solved_ref, sums_ref, *refs):
            rounded_above = refs[:above]
            matrices = refs[above:-4]
            result_ref, rounded_ref, keep_ref, give_ref = refs[-4:]
            corrected = solved_ref[...] - jnp.sum(sums_ref[...], axis=0)
            result = solve_backward(level, live_ref, inverse_ref, corrected)
            result_ref[...] = result
            rounded = result.astype(bf16)
            rounded_ref[...] = rounded
            solved = {level: rounded}
            for index in range(above):
                solved[level + 1 + index] = rounded_above[index][...]
            backward_partials(keep_ref, give_ref, solved, level - 1, matrices)

        return body

    def last(live_ref, inverse_ref, solved_ref, sums_ref, *refs):
        out_ref = refs[-1]
        corrected = solved_ref[...] - jnp.sum(sums_ref[...], axis=0)
        out_ref[0] = solve_backward(0, live_ref, inverse_ref, corrected)
        for level in range(1, levels):
            out_ref[level] = refs[level - 1][...]

    def exchange(own):
        shifted = [own]
        for shift in range(1, col_parts):
            to_lower = [((q + shift) % col_parts, q) for q in range(col_parts)]
            shifted.append(lax.ppermute(own, "col", to_lower))
        return shifted

    def trade_beside(blocks, group):
        moved = exchange(masked[group]) if group < len(groups) else None
        blocks = trade(blocks)
        for later in range(group + 1, len(groups)):
            masked[later], blocks = lax.optimization_barrier((masked[later], blocks))
        return blocks, moved

    solved, gathered, held = [], [], []
    shaped = lambda *shape: jax.ShapeDtypeStruct(shape, f32)
    with jax.named_scope("forward_first"):
        operands = [
            pltpu.with_memory_space_constraint(x, pltpu.HBM)
            for x in (right_sides, factors, pattern, live_widths.reshape(1, levels), inverses)
        ]
        value, out, right_sides, live, inverses, *masked = call(
            first,
            (block_f32, spread_bf16, shaped(levels, rhs, width), shaped(levels, 1, width), shaped(levels, width, width))
            + tuple(jax.ShapeDtypeStruct((len(group), width, local_cols), bf16) for group in groups),
            *operands,
            space=pltpu.HBM,
            scratch=[
                pltpu.VMEM(factors.shape, bf16),
                pltpu.VMEM(pattern.shape, jnp.int32),
                pltpu.VMEM((1, levels), jnp.int32),
                pltpu.SemaphoreType.DMA((4 + pairs,)),
            ],
        )
    solved.append(value)
    blocks, moved = trade_beside(out, 0)
    gathered.append(blocks)
    held.append(moved)
    for level in range(1, levels - 1):
        with jax.named_scope("forward_level"):
            value, out = call(middle(level), (block_f32, spread_bf16), live, right_sides, inverses, *gathered, *flat(held))
        solved.append(value)
        blocks, moved = trade_beside(out, level)
        gathered.append(blocks)
        if moved is not None:
            held.append(moved)
    results, rounded = {}, {}
    level = levels - 1
    with jax.named_scope("top_level"):
        results[level], rounded[level], *halves = call(
            top, (block_f32, block_bf16, twins_f32, twins_f32), live, right_sides, inverses, *gathered, *flat(held)
        )
    sums = scatter(*halves)
    for level in range(levels - 2, 0, -1):
        with jax.named_scope("backward_level"):
            results[level], rounded[level], *halves = call(
                down(level),
                (block_f32, block_bf16, twins_f32, twins_f32),
                live,
                inverses,
                solved[level],
                sums,
                *[rounded[upper] for upper in range(level + 1, levels)],
                *flat(held),
            )
        sums = scatter(*halves)
    with jax.named_scope("backward_last"):
        return call(
            last,
            jax.ShapeDtypeStruct((levels, rhs, width), f32),
            live,
            inverses,
            solved[0],
            sums,
            *[results[level] for level in range(1, levels)],
        )


def solution(mesh):
    parts = (mesh.shape["row"], mesh.shape["col"])

    def run(*operands):
        return local(parts, *operands)

    return jax.shard_map(
        run,
        mesh=mesh,
        in_specs=(
            P(None, "col", "row"),
            P(None, "row", "col"),
            P(None, "row", "col"),
            P(None, "row"),
            P(None, "row", None, None),
        ),
        out_specs=P(None, "col", "row"),
        check_vma=False,
    )
```

```python
import math

import jax
import jax.numpy as jnp
from jax import lax
from jax.experimental import pallas as pl
from jax.experimental.pallas import tpu as pltpu
from jax.sharding import PartitionSpec as P

HIGHEST = lax.Precision.HIGHEST


def pair_lookup(level_count):
    lookup = {}
    for lower_level in range(level_count):
        for above_level in range(lower_level + 1, level_count):
            lookup[above_level, lower_level] = len(lookup)
    return lookup


def call(kernel, outs, *operands, space=pltpu.VMEM, spaces=None, scratch=()):
    return pl.pallas_call(
        kernel,
        out_shape=outs,
        in_specs=[pl.BlockSpec(memory_space=s) for s in (spaces or [space] * len(operands))],
        out_specs=jax.tree.map(lambda _: pl.BlockSpec(memory_space=pltpu.VMEM), outs),
        scratch_shapes=scratch,
        compiler_params=pltpu.CompilerParams(vmem_limit_bytes=48 * 1024 * 1024),
    )(*operands)


def local(parts, right_sides, factors, pattern, live_widths, inverses):
    row_parts, col_parts = parts
    levels, rhs, width = right_sides.shape
    pairs, _, local_cols = factors.shape
    half = local_cols // width
    total_blocks = half * col_parts
    lookup = pair_lookup(levels)
    needed = [lookup[level, lower] for level in range(1, levels) for lower in range(level)]
    group_size = -(-pairs // (levels - 1))
    groups = [needed[k : k + group_size] for k in range(0, pairs, group_size)]
    place_of = {pair: (g, k) for g, group in enumerate(groups) for k, pair in enumerate(group)}
    inverses = inverses.reshape(levels, width, width)
    f32, bf16 = jnp.float32, jnp.bfloat16

    block_f32 = jax.ShapeDtypeStruct((rhs, width), f32)
    block_bf16 = jax.ShapeDtypeStruct((rhs, width), bf16)
    spread_bf16 = jax.ShapeDtypeStruct((total_blocks, rhs, width), bf16)
    twins = row_parts // 2
    twins_f32 = jax.ShapeDtypeStruct((twins, rhs, width), f32)

    middle_row = row_parts // 2 + 1
    row_order = [middle_row] + [k for k in range(0, row_parts, 2)] + [k for k in range(1, row_parts, 2) if k != middle_row]
    step = next(s for s in range(5, 5 + twins) if math.gcd(s, twins) == 1)
    twin_order = [(twins // 2 + step * k) % twins for k in range(twins)]

    def row_place(index):
        odd_place = twins + index // 2 + jnp.where(index < middle_row, 1, 0)
        odd_place = jnp.where(index == middle_row, 0, odd_place)
        return jnp.where(lax.rem(index, 2) == 0, 1 + index // 2, odd_place)

    def trade(blocks):
        return lax.all_to_all(blocks, "row", 0, 0, axis_index_groups=[row_order])

    def scatter(keep, give):
        taken = lax.ppermute(give, "row", [(k, k ^ 1) for k in range(row_parts)])
        with jax.named_scope("sum_twins"):
            sums = call(add, twins_f32, keep, taken)
        one_of_each = [[2 * g + (g + side) % 2 for g in twin_order] for side in (1, 0)]
        return lax.all_to_all(sums, "row", 0, 0, axis_index_groups=one_of_each)

    def solve_forward(level, live_ref, rhs_ref, inverse_ref, total):
        live = live_ref[level]
        vector = (rhs_ref[level] - total) * live
        product = lax.dot_general(
            vector, inverse_ref[level], (((1,), (1,)), ((), ())), precision=HIGHEST, preferred_element_type=f32
        )
        return product * live

    def solve_backward(level, live_ref, inverse_ref, corrected):
        live = live_ref[level]
        product = lax.dot_general(
            corrected * live, inverse_ref[level], (((1,), (0,)), ((), ())), precision=HIGHEST, preferred_element_type=f32
        )
        return product * live

    def forward_total(gathered, level, matrices):
        mine = lax.axis_index("col")
        total = None
        for shift in range(col_parts):
            start = lax.rem(mine + shift, col_parts) * half
            for lower in range(level):
                left = jnp.concatenate([gathered[lower][row_place(start + k)] for k in range(half)], axis=1)
                term = lax.dot_general(
                    left, matrix(matrices, level, lower, shift), (((1,), (1,)), ((), ())), preferred_element_type=f32
                )
                total = term if total is None else total + term
        return total

    def add(left_ref, right_ref, out_ref):
        for place, g in enumerate(twin_order):
            out_ref[place] = left_ref[g] + right_ref[g]

    def backward_partials(keep_ref, give_ref, solved, lower, matrices):
        mine = lax.axis_index("col")
        index = lax.axis_index("row")
        for shift in range(col_parts):
            start = lax.rem(mine + shift, col_parts) * half
            total = None
            for level, vector in solved.items():
                term = lax.dot_general(
                    vector, matrix(matrices, level, lower, shift), (((1,), (0,)), ((), ())), preferred_element_type=f32
                )
                total = term if total is None else total + term
            for block in range(0, half, 2):
                even = total[:, block * width : (block + 1) * width]
                uneven = total[:, (block + 1) * width : (block + 2) * width]
                g = start // 2 + block // 2
                odd = lax.rem(index + index // 2 + g, 2) == 1
                keep_ref[g] = jnp.where(odd, uneven, even)
                give_ref[g] = jnp.where(odd, even, uneven)

    def spread(out_ref, value):
        out_ref[...] = jnp.broadcast_to(value.astype(bf16)[None], out_ref.shape)

    def mask_pair(out_ref, place, pattern_ref, factor_ref, pair):
        for block in range(half):
            columns = slice(block * width, (block + 1) * width)
            kept = jnp.broadcast_to(pattern_ref[pair][:, block : block + 1].astype(f32), (width, width))
            out_ref[place, :, columns] = factor_ref[pair, :, columns] * kept.astype(bf16)

    def first_mask(factor_hbm, pattern_hbm, masked_ref, pattern_out, factor_ref, pattern_ref, sems):
        order = groups[0]
        small = [pltpu.make_async_copy(pattern_hbm, pattern_ref, sems.at[0])]
        large = [
            pltpu.make_async_copy(factor_hbm.at[pair], factor_ref.at[pair], sems.at[1 + k])
            for k, pair in enumerate(order)
        ]
        for copy in small + large:
            copy.start()
        for copy in small:
            copy.wait()
        pattern_out[...] = pattern_ref[...]
        for copy, pair in zip(large, order):
            copy.wait()
            group, place = place_of[pair]
            mask_pair(masked_ref, place, pattern_ref, factor_ref, pair)

    def first(
        rhs_hbm, factor_hbm, pattern_ref, widths_hbm, inverse_hbm,
        solved_ref, out_ref, rhs_ref, live_ref, inverse_ref, *refs,
    ):
        masked_refs = [None, *refs[: len(groups) - 1]]
        factor_ref, widths_ref, sems = refs[len(groups) - 1 :]
        order = needed[len(groups[0]) :]
        small = [
            pltpu.make_async_copy(widths_hbm, widths_ref, sems.at[1]),
            pltpu.make_async_copy(rhs_hbm, rhs_ref, sems.at[2]),
            pltpu.make_async_copy(inverse_hbm, inverse_ref, sems.at[3]),
        ]
        large = [
            pltpu.make_async_copy(factor_hbm.at[pair], factor_ref.at[pair], sems.at[4 + k])
            for k, pair in enumerate(order)
        ]
        for copy in small + large:
            copy.start()
        for copy in small:
            copy.wait()
        column = lax.broadcasted_iota(jnp.int32, (1, width), 1)
        for level in range(levels):
            live_ref[level] = (column < widths_ref[:, level : level + 1]).astype(f32)
        value = solve_forward(0, live_ref, rhs_ref, inverse_ref, jnp.zeros((rhs, width), f32))
        solved_ref[...] = value
        spread(out_ref, value)
        for copy, pair in zip(large, order):
            copy.wait()
            group, place = place_of[pair]
            mask_pair(masked_refs[group], place, pattern_ref, factor_ref, pair)

    def flat(held):
        return [m for moved in held for m in moved]

    def matrix(refs, level, lower, shift):
        group, place = place_of[lookup[level, lower]]
        return refs[group * col_parts + shift][place]

    def middle(level):
        def body(live_ref, rhs_ref, inverse_ref, *refs):
            gathered, matrices = refs[:level], refs[level:-2]
            solved_ref, out_ref = refs[-2:]
            total = forward_total(gathered, level, matrices)
            value = solve_forward(level, live_ref, rhs_ref, inverse_ref, total)
            solved_ref[...] = value
            spread(out_ref, value)

        return body

    def top(live_ref, rhs_ref, inverse_ref, *refs):
        level = levels - 1
        gathered, matrices = refs[:level], refs[level:-4]
        result_ref, rounded_ref, keep_ref, give_ref = refs[-4:]
        total = forward_total(gathered, level, matrices)
        value = solve_forward(level, live_ref, rhs_ref, inverse_ref, total)
        result = solve_backward(level, live_ref, inverse_ref, value)
        result_ref[...] = result
        rounded = result.astype(bf16)
        rounded_ref[...] = rounded
        backward_partials(keep_ref, give_ref, {level: rounded}, level - 1, matrices)

    def down(level):
        above = levels - 1 - level

        def body(live_ref, inverse_ref, solved_ref, sums_ref, *refs):
            rounded_above = refs[:above]
            matrices = refs[above:-4]
            result_ref, rounded_ref, keep_ref, give_ref = refs[-4:]
            corrected = solved_ref[...] - jnp.sum(sums_ref[...], axis=0)
            result = solve_backward(level, live_ref, inverse_ref, corrected)
            result_ref[...] = result
            rounded = result.astype(bf16)
            rounded_ref[...] = rounded
            solved = {level: rounded}
            for index in range(above):
                solved[level + 1 + index] = rounded_above[index][...]
            backward_partials(keep_ref, give_ref, solved, level - 1, matrices)

        return body

    def last(live_ref, inverse_ref, solved_ref, sums_ref, *refs):
        out_ref = refs[-1]
        corrected = solved_ref[...] - jnp.sum(sums_ref[...], axis=0)
        out_ref[0] = solve_backward(0, live_ref, inverse_ref, corrected)
        for level in range(1, levels):
            out_ref[level] = refs[level - 1][...]

    def exchange(own):
        shifted = [own]
        for shift in range(1, col_parts):
            to_lower = [((q + shift) % col_parts, q) for q in range(col_parts)]
            shifted.append(lax.ppermute(own, "col", to_lower))
        return shifted

    def trade_beside(blocks, group):
        moved = exchange(masked[group]) if group < len(groups) else None
        blocks = trade(blocks)
        for later in range(group + 1, len(groups)):
            masked[later], blocks = lax.optimization_barrier((masked[later], blocks))
        return blocks, moved

    solved, gathered, held = [], [], []
    shaped = lambda *shape: jax.ShapeDtypeStruct(shape, f32)
    with jax.named_scope("forward_first"):
        operands = [
            pltpu.with_memory_space_constraint(x, pltpu.HBM)
            for x in (right_sides, factors, pattern, live_widths.reshape(1, levels), inverses)
        ]
        masked0, pattern_vmem = call(first_mask,
            (jax.ShapeDtypeStruct((len(groups[0]), width, local_cols), bf16), jax.ShapeDtypeStruct(pattern.shape, jnp.int32)),
            operands[1], operands[2], space=pltpu.HBM,
            scratch=[
                pltpu.VMEM(factors.shape, bf16),
                pltpu.VMEM(pattern.shape, jnp.int32),
                pltpu.SemaphoreType.DMA((1 + pairs,)),
            ],
        )
        operands[2] = pattern_vmem
        value, out, right_sides, live, inverses, *masked = call(
            first,
            (block_f32, spread_bf16, shaped(levels, rhs, width), shaped(levels, 1, width), shaped(levels, width, width))
            + tuple(jax.ShapeDtypeStruct((len(group), width, local_cols), bf16) for group in groups[1:]),
            *operands,
            spaces=[pltpu.HBM, pltpu.HBM, pltpu.VMEM, pltpu.HBM, pltpu.HBM],
            scratch=[
                pltpu.VMEM(factors.shape, bf16),
                pltpu.VMEM((1, levels), jnp.int32),
                pltpu.SemaphoreType.DMA((4 + pairs,)),
            ],
        )
        masked = [masked0, *masked]
    solved.append(value)
    blocks, moved = trade_beside(out, 0)
    gathered.append(blocks)
    held.append(moved)
    for level in range(1, levels - 1):
        with jax.named_scope("forward_level"):
            value, out = call(middle(level), (block_f32, spread_bf16), live, right_sides, inverses, *gathered, *flat(held))
        solved.append(value)
        blocks, moved = trade_beside(out, level)
        gathered.append(blocks)
        if moved is not None:
            held.append(moved)
    results, rounded = {}, {}
    level = levels - 1
    with jax.named_scope("top_level"):
        results[level], rounded[level], *halves = call(
            top, (block_f32, block_bf16, twins_f32, twins_f32), live, right_sides, inverses, *gathered, *flat(held)
        )
    sums = scatter(*halves)
    for level in range(levels - 2, 0, -1):
        with jax.named_scope("backward_level"):
            results[level], rounded[level], *halves = call(
                down(level),
                (block_f32, block_bf16, twins_f32, twins_f32),
                live,
                inverses,
                solved[level],
                sums,
                *[rounded[upper] for upper in range(level + 1, levels)],
                *flat(held),
            )
        sums = scatter(*halves)
    with jax.named_scope("backward_last"):
        return call(
            last,
            jax.ShapeDtypeStruct((levels, rhs, width), f32),
            live,
            inverses,
            solved[0],
            sums,
            *[results[level] for level in range(1, levels)],
        )


def solution(mesh):
    parts = (mesh.shape["row"], mesh.shape["col"])

    def run(*operands):
        return local(parts, *operands)

    return jax.shard_map(
        run,
        mesh=mesh,
        in_specs=(
            P(None, "col", "row"),
            P(None, "row", "col"),
            P(None, "row", "col"),
            P(None, "row"),
            P(None, "row", None, None),
        ),
        out_specs=P(None, "col", "row"),
        check_vma=False,
    )
```

```python
import math

import jax
import jax.numpy as jnp
from jax import lax
from jax.experimental import pallas as pl
from jax.experimental.pallas import tpu as pltpu
from jax.sharding import PartitionSpec as P

HIGHEST = lax.Precision.HIGHEST


def pair_lookup(level_count):
    lookup = {}
    for lower_level in range(level_count):
        for above_level in range(lower_level + 1, level_count):
            lookup[above_level, lower_level] = len(lookup)
    return lookup


def call(kernel, outs, *operands, space=pltpu.VMEM, spaces=None, scratch=()):
    return pl.pallas_call(
        kernel,
        out_shape=outs,
        in_specs=[pl.BlockSpec(memory_space=s) for s in (spaces or [space] * len(operands))],
        out_specs=jax.tree.map(lambda _: pl.BlockSpec(memory_space=pltpu.VMEM), outs),
        scratch_shapes=scratch,
        compiler_params=pltpu.CompilerParams(vmem_limit_bytes=48 * 1024 * 1024),
    )(*operands)


def local(parts, right_sides, factors, pattern, live_widths, inverses):
    row_parts, col_parts = parts
    levels, rhs, width = right_sides.shape
    pairs, _, local_cols = factors.shape
    half = local_cols // width
    total_blocks = half * col_parts
    lookup = pair_lookup(levels)
    needed = [lookup[level, lower] for level in range(1, levels) for lower in range(level)]
    group_size = -(-pairs // (levels - 1))
    groups = [needed[k : k + group_size] for k in range(0, pairs, group_size)]
    place_of = {pair: (g, k) for g, group in enumerate(groups) for k, pair in enumerate(group)}
    inverses = inverses.reshape(levels, width, width)
    f32, bf16 = jnp.float32, jnp.bfloat16

    block_f32 = jax.ShapeDtypeStruct((rhs, width), f32)
    block_bf16 = jax.ShapeDtypeStruct((rhs, width), bf16)
    spread_bf16 = jax.ShapeDtypeStruct((total_blocks, rhs, width), bf16)
    twins = row_parts // 2
    twins_f32 = jax.ShapeDtypeStruct((twins, rhs, width), f32)

    middle_row = row_parts // 2 + 1
    row_order = [middle_row] + [k for k in range(0, row_parts, 2)] + [k for k in range(1, row_parts, 2) if k != middle_row]
    step = next(s for s in range(5, 5 + twins) if math.gcd(s, twins) == 1)
    twin_order = [(twins // 2 + step * k) % twins for k in range(twins)]

    def row_place(index):
        odd_place = twins + index // 2 + jnp.where(index < middle_row, 1, 0)
        odd_place = jnp.where(index == middle_row, 0, odd_place)
        return jnp.where(lax.rem(index, 2) == 0, 1 + index // 2, odd_place)

    def trade(blocks):
        return lax.all_to_all(blocks, "row", 0, 0, axis_index_groups=[row_order])

    def scatter(keep, give, early=None):
        taken = lax.ppermute(give, "row", [(k, k ^ 1) for k in range(row_parts)])
        begun = early() if early else ()
        with jax.named_scope("sum_twins"):
            sums = call(add, twins_f32, keep, taken)
        sums, begun = lax.optimization_barrier((sums, begun))
        one_of_each = [[2 * g + (g + side) % 2 for g in twin_order] for side in (1, 0)]
        return lax.all_to_all(sums, "row", 0, 0, axis_index_groups=one_of_each), begun

    def solve_forward(level, live_ref, rhs_ref, inverse_ref, total):
        live = live_ref[level]
        vector = (rhs_ref[level] - total) * live
        product = lax.dot_general(
            vector, inverse_ref[level], (((1,), (1,)), ((), ())), precision=HIGHEST, preferred_element_type=f32
        )
        return product * live

    def solve_backward(level, live_ref, inverse_ref, corrected):
        live = live_ref[level]
        product = lax.dot_general(
            corrected * live, inverse_ref[level], (((1,), (0,)), ((), ())), precision=HIGHEST, preferred_element_type=f32
        )
        return product * live

    def forward_total(gathered, level, matrices):
        mine = lax.axis_index("col")
        total = None
        for shift in range(col_parts):
            start = lax.rem(mine + shift, col_parts) * half
            for lower in range(level):
                left = jnp.concatenate([gathered[lower][row_place(start + k)] for k in range(half)], axis=1)
                term = lax.dot_general(
                    left, matrix(matrices, level, lower, shift), (((1,), (1,)), ((), ())), preferred_element_type=f32
                )
                total = term if total is None else total + term
        return total

    def add(left_ref, right_ref, out_ref):
        for place, g in enumerate(twin_order):
            out_ref[place] = left_ref[g] + right_ref[g]

    def backward_partials(keep_ref, give_ref, solved, lower, matrices, begun=None):
        mine = lax.axis_index("col")
        index = lax.axis_index("row")
        for shift in range(col_parts):
            start = lax.rem(mine + shift, col_parts) * half
            total = None
            for level, vector in solved.items():
                term = lax.dot_general(
                    vector, matrix(matrices, level, lower, shift), (((1,), (0,)), ((), ())), preferred_element_type=f32
                )
                total = term if total is None else total + term
            for block in range(0, half, 2):
                even = total[:, block * width : (block + 1) * width]
                uneven = total[:, (block + 1) * width : (block + 2) * width]
                g = start // 2 + block // 2
                kept, given = (0.0, 0.0) if begun is None else (begun[0][g], begun[1][g])
                odd = lax.rem(index + index // 2 + g, 2) == 1
                keep_ref[g] = jnp.where(odd, uneven, even) + kept
                give_ref[g] = jnp.where(odd, even, uneven) + given

    def spread(out_ref, value):
        out_ref[...] = jnp.broadcast_to(value.astype(bf16)[None], out_ref.shape)

    def mask_pair(out_ref, place, pattern_ref, factor_ref, pair):
        for block in range(half):
            columns = slice(block * width, (block + 1) * width)
            kept = jnp.broadcast_to(pattern_ref[pair][:, block : block + 1].astype(f32), (width, width))
            out_ref[place, :, columns] = factor_ref[pair, :, columns] * kept.astype(bf16)

    def first_mask(factor_hbm, pattern_hbm, masked_ref, pattern_out, factor_ref, pattern_ref, sems):
        order = groups[0]
        small = [pltpu.make_async_copy(pattern_hbm, pattern_ref, sems.at[0])]
        large = [
            pltpu.make_async_copy(factor_hbm.at[pair], factor_ref.at[pair], sems.at[1 + k])
            for k, pair in enumerate(order)
        ]
        for copy in small + large:
            copy.start()
        for copy in small:
            copy.wait()
        pattern_out[...] = pattern_ref[...]
        for copy, pair in zip(large, order):
            copy.wait()
            group, place = place_of[pair]
            mask_pair(masked_ref, place, pattern_ref, factor_ref, pair)

    def first(
        rhs_hbm, factor_hbm, pattern_ref, widths_hbm, inverse_hbm,
        solved_ref, out_ref, rhs_ref, live_ref, inverse_ref, *refs,
    ):
        masked_refs = [None, *refs[: len(groups) - 1]]
        factor_ref, widths_ref, sems = refs[len(groups) - 1 :]
        order = needed[len(groups[0]) :]
        small = [
            pltpu.make_async_copy(widths_hbm, widths_ref, sems.at[1]),
            pltpu.make_async_copy(rhs_hbm, rhs_ref, sems.at[2]),
            pltpu.make_async_copy(inverse_hbm, inverse_ref, sems.at[3]),
        ]
        large = [
            pltpu.make_async_copy(factor_hbm.at[pair], factor_ref.at[pair], sems.at[4 + k])
            for k, pair in enumerate(order)
        ]
        for copy in small + large:
            copy.start()
        for copy in small:
            copy.wait()
        column = lax.broadcasted_iota(jnp.int32, (1, width), 1)
        for level in range(levels):
            live_ref[level] = (column < widths_ref[:, level : level + 1]).astype(f32)
        value = solve_forward(0, live_ref, rhs_ref, inverse_ref, jnp.zeros((rhs, width), f32))
        solved_ref[...] = value
        spread(out_ref, value)
        for copy, pair in zip(large, order):
            copy.wait()
            group, place = place_of[pair]
            mask_pair(masked_refs[group], place, pattern_ref, factor_ref, pair)

    def flat(held):
        return [m for moved in held for m in moved]

    def matrix(refs, level, lower, shift):
        group, place = place_of[lookup[level, lower]]
        return refs[group * col_parts + shift][place]

    def middle(level):
        def body(live_ref, rhs_ref, inverse_ref, *refs):
            gathered, matrices = refs[:level], refs[level:-2]
            solved_ref, out_ref = refs[-2:]
            total = forward_total(gathered, level, matrices)
            value = solve_forward(level, live_ref, rhs_ref, inverse_ref, total)
            solved_ref[...] = value
            spread(out_ref, value)

        return body

    def top(live_ref, rhs_ref, inverse_ref, *refs):
        level = levels - 1
        gathered, matrices = refs[:level], refs[level:-4]
        result_ref, rounded_ref, keep_ref, give_ref = refs[-4:]
        total = forward_total(gathered, level, matrices)
        value = solve_forward(level, live_ref, rhs_ref, inverse_ref, total)
        result = solve_backward(level, live_ref, inverse_ref, value)
        result_ref[...] = result
        rounded = result.astype(bf16)
        rounded_ref[...] = rounded
        backward_partials(keep_ref, give_ref, {level: rounded}, level - 1, matrices)

    def backward_early(lower):
        known = range(lower + 2, levels)

        def body(*refs):
            solved = {level: refs[k][...] for k, level in enumerate(known)}
            matrices, (keep_ref, give_ref) = refs[len(known) : -2], refs[-2:]
            backward_partials(keep_ref, give_ref, solved, lower, matrices)

        return body

    def down(level):
        def body(live_ref, inverse_ref, solved_ref, sums_ref, early_keep_ref, early_give_ref, *refs):
            outs = 3 + (level > 1)
            matrices = refs[:-outs]
            keep_ref, give_ref, result_ref = refs[-outs:][:3]
            corrected = solved_ref[...] - jnp.sum(sums_ref[...], axis=0)
            result = solve_backward(level, live_ref, inverse_ref, corrected)
            result_ref[...] = result
            rounded = result.astype(bf16)
            if level > 1:
                refs[-1][...] = rounded
            begun = early_keep_ref, early_give_ref
            backward_partials(keep_ref, give_ref, {level: rounded}, level - 1, matrices, begun)

        return body

    def last(live_ref, inverse_ref, solved_ref, sums_ref, *refs):
        out_ref = refs[-1]
        corrected = solved_ref[...] - jnp.sum(sums_ref[...], axis=0)
        out_ref[0] = solve_backward(0, live_ref, inverse_ref, corrected)
        for level in range(1, levels):
            out_ref[level] = refs[level - 1][...]

    def exchange(own):
        shifted = [own]
        for shift in range(1, col_parts):
            to_lower = [((q + shift) % col_parts, q) for q in range(col_parts)]
            shifted.append(lax.ppermute(own, "col", to_lower))
        return shifted

    def trade_beside(blocks, group):
        moved = exchange(masked[group]) if group < len(groups) else None
        blocks = trade(blocks)
        for later in range(group + 1, len(groups)):
            masked[later], blocks = lax.optimization_barrier((masked[later], blocks))
        return blocks, moved

    solved, gathered, held = [], [], []
    shaped = lambda *shape: jax.ShapeDtypeStruct(shape, f32)
    with jax.named_scope("forward_first"):
        operands = [
            pltpu.with_memory_space_constraint(x, pltpu.HBM)
            for x in (right_sides, factors, pattern, live_widths.reshape(1, levels), inverses)
        ]
        masked0, pattern_vmem = call(first_mask,
            (jax.ShapeDtypeStruct((len(groups[0]), width, local_cols), bf16), jax.ShapeDtypeStruct(pattern.shape, jnp.int32)),
            operands[1], operands[2], space=pltpu.HBM,
            scratch=[
                pltpu.VMEM(factors.shape, bf16),
                pltpu.VMEM(pattern.shape, jnp.int32),
                pltpu.SemaphoreType.DMA((1 + pairs,)),
            ],
        )
        operands[2] = pattern_vmem
        value, out, right_sides, live, inverses, *masked = call(
            first,
            (block_f32, spread_bf16, shaped(levels, rhs, width), shaped(levels, 1, width), shaped(levels, width, width))
            + tuple(jax.ShapeDtypeStruct((len(group), width, local_cols), bf16) for group in groups[1:]),
            *operands,
            spaces=[pltpu.HBM, pltpu.HBM, pltpu.VMEM, pltpu.HBM, pltpu.HBM],
            scratch=[
                pltpu.VMEM(factors.shape, bf16),
                pltpu.VMEM((1, levels), jnp.int32),
                pltpu.SemaphoreType.DMA((4 + pairs,)),
            ],
        )
        masked = [masked0, *masked]
    solved.append(value)
    blocks, moved = trade_beside(out, 0)
    gathered.append(blocks)
    held.append(moved)
    for level in range(1, levels - 1):
        with jax.named_scope("forward_level"):
            value, out = call(middle(level), (block_f32, spread_bf16), live, right_sides, inverses, *gathered, *flat(held))
        solved.append(value)
        blocks, moved = trade_beside(out, level)
        gathered.append(blocks)
        if moved is not None:
            held.append(moved)
    factors = flat(held)
    results, rounded = {}, {}
    level = levels - 1
    with jax.named_scope("top_level"):
        results[level], rounded[level], *halves = call(
            top, (block_f32, block_bf16, twins_f32, twins_f32), live, right_sides, inverses, *gathered, *factors
        )

    def begin(lower):
        with jax.named_scope("backward_early"):
            known = [rounded[level] for level in range(lower + 2, levels)]
            return call(backward_early(lower), (twins_f32, twins_f32), *known, *factors)

    for level in range(levels - 2, 0, -1):
        sums, begun = scatter(*halves, lambda: begin(level - 1))
        with jax.named_scope("backward_level"):
            keep, give, results[level], *rest = call(
                down(level),
                (twins_f32, twins_f32, block_f32) + (block_bf16,) * (level > 1),
                live,
                inverses,
                solved[level],
                sums,
                *begun,
                *factors,
            )
        halves = keep, give
        rounded[level] = rest[0] if rest else None
    sums, _ = scatter(*halves)
    with jax.named_scope("backward_last"):
        return call(
            last,
            jax.ShapeDtypeStruct((levels, rhs, width), f32),
            live,
            inverses,
            solved[0],
            sums,
            *[results[level] for level in range(1, levels)],
        )


def solution(mesh):
    parts = (mesh.shape["row"], mesh.shape["col"])

    def run(*operands):
        return local(parts, *operands)

    return jax.shard_map(
        run,
        mesh=mesh,
        in_specs=(
            P(None, "col", "row"),
            P(None, "row", "col"),
            P(None, "row", "col"),
            P(None, "row"),
            P(None, "row", None, None),
        ),
        out_specs=P(None, "col", "row"),
        check_vma=False,
    )
```

```python
import math

import jax
import jax.numpy as jnp
from jax import lax
from jax.experimental import pallas as pl
from jax.experimental.pallas import tpu as pltpu
from jax.sharding import PartitionSpec as P

HIGHEST = lax.Precision.HIGHEST


def pair_lookup(level_count):
    lookup = {}
    for lower_level in range(level_count):
        for above_level in range(lower_level + 1, level_count):
            lookup[above_level, lower_level] = len(lookup)
    return lookup


def call(kernel, outs, *operands, space=pltpu.VMEM, spaces=None, scratch=()):
    return pl.pallas_call(
        kernel,
        out_shape=outs,
        in_specs=[pl.BlockSpec(memory_space=s) for s in (spaces or [space] * len(operands))],
        out_specs=jax.tree.map(lambda _: pl.BlockSpec(memory_space=pltpu.VMEM), outs),
        scratch_shapes=scratch,
        compiler_params=pltpu.CompilerParams(vmem_limit_bytes=48 * 1024 * 1024),
    )(*operands)


def local(parts, right_sides, factors, pattern, live_widths, inverses):
    row_parts, col_parts = parts
    levels, rhs, width = right_sides.shape
    pairs, _, local_cols = factors.shape
    half = local_cols // width
    total_blocks = half * col_parts
    lookup = pair_lookup(levels)
    needed = [lookup[level, lower] for level in range(1, levels) for lower in range(level)]
    group_size = -(-pairs // (levels - 1))
    groups = [needed[k : k + group_size] for k in range(0, pairs, group_size)]
    place_of = {pair: (g, k) for g, group in enumerate(groups) for k, pair in enumerate(group)}
    inverses = inverses.reshape(levels, width, width)
    f32, bf16 = jnp.float32, jnp.bfloat16

    def shaped(*shape):
        return jax.ShapeDtypeStruct(shape, f32)

    block_f32 = jax.ShapeDtypeStruct((rhs, width), f32)
    block_bf16 = jax.ShapeDtypeStruct((rhs, width), bf16)
    spread_bf16 = jax.ShapeDtypeStruct((total_blocks, rhs, width), bf16)
    twins = row_parts // 2
    twins_f32 = jax.ShapeDtypeStruct((twins, rhs, width), f32)

    middle_row = 2 * (twins // 2 + 1) + 1
    row_order = [middle_row] + [k for k in range(0, row_parts, 2)] + [k for k in range(1, row_parts, 2) if k != middle_row]
    step = next(s for s in range(5, 5 + twins) if math.gcd(s, twins) == 1)
    twin_orders = [[(root + step * k) % twins for k in range(twins)] for root in (twins // 2, twins // 2 + 1)]

    def row_place(index):
        odd_place = twins + index // 2 + jnp.where(index < middle_row, 1, 0)
        odd_place = jnp.where(index == middle_row, 0, odd_place)
        return jnp.where(lax.rem(index, 2) == 0, 1 + index // 2, odd_place)

    def trade(blocks):
        return lax.all_to_all(blocks, "row", 0, 0, axis_index_groups=[row_order])

    def scatter(keep, give, early=None):
        taken = lax.ppermute(give, "row", [(k, k ^ 1) for k in range(row_parts)])
        begun = early() if early else ()
        with jax.named_scope("sum_twins"):
            sums = call(add, twins_f32, keep, taken)
        sums, begun = lax.optimization_barrier((sums, begun))
        one_of_each = [[2 * g + (g + side) % 2 for g in order] for side, order in zip((1, 0), twin_orders)]
        return lax.all_to_all(sums, "row", 0, 0, axis_index_groups=one_of_each), begun

    left_parts, right_parts = (0, 0, 1, 0, 1, 2), (0, 1, 0, 2, 1, 0)
    deep = len(left_parts) * width
    forward_slot = {level: level - 1 for level in range(1, levels - 1)}
    top_slot = levels - 2
    backward_slot = {level: levels - 1 + level for level in range(levels - 1)}
    slots = 2 * levels - 2

    def split(value):
        parts = []
        for _ in range(3):
            parts.append(value.astype(bf16))
            value = value - parts[-1].astype(f32)
        return parts

    def store_solver(solver_ref, slot, matrix):
        parts = split(matrix)
        for k, part in enumerate(right_parts):
            solver_ref[slot, k * width : (k + 1) * width, :] = parts[part]

    def solve(solver_ref, slot, vector):
        parts = split(vector)
        left = jnp.concatenate([parts[part] for part in left_parts], axis=1)
        return lax.dot_general(left, solver_ref[slot], (((1,), (0,)), ((), ())), preferred_element_type=f32)

    def forward_total(gathered, level, matrices):
        mine = lax.axis_index("col")
        total = None
        for shift in range(col_parts):
            start = lax.rem(mine + shift, col_parts) * half
            for lower in range(level):
                left = jnp.concatenate([gathered[lower][row_place(start + k)] for k in range(half)], axis=1)
                term = lax.dot_general(
                    left, matrix(matrices, level, lower, shift), (((1,), (1,)), ((), ())), preferred_element_type=f32
                )
                total = term if total is None else total + term
        return total

    def add(left_ref, right_ref, out_ref):
        index = lax.axis_index("row")
        second = lax.rem(index + index // 2, 2) == 0
        for place in range(twins):
            g = jnp.where(second, twin_orders[1][place], twin_orders[0][place])
            out_ref[place] = left_ref[g] + right_ref[g]

    def backward_partials(keep_ref, give_ref, solved, lower, matrices, begun=None):
        mine = lax.axis_index("col")
        index = lax.axis_index("row")
        for shift in range(col_parts):
            start = lax.rem(mine + shift, col_parts) * half
            total = None
            for level, vector in solved.items():
                term = lax.dot_general(
                    vector, matrix(matrices, level, lower, shift), (((1,), (0,)), ((), ())), preferred_element_type=f32
                )
                total = term if total is None else total + term
            for block in range(0, half, 2):
                even = total[:, block * width : (block + 1) * width]
                uneven = total[:, (block + 1) * width : (block + 2) * width]
                g = start // 2 + block // 2
                kept, given = (0.0, 0.0) if begun is None else (begun[0][g], begun[1][g])
                odd = lax.rem(index + index // 2 + g, 2) == 1
                keep_ref[g] = jnp.where(odd, uneven, even) + kept
                give_ref[g] = jnp.where(odd, even, uneven) + given

    def spread(out_ref, value):
        out_ref[...] = jnp.broadcast_to(value.astype(bf16)[None], out_ref.shape)

    def mask_pair(out_ref, place, pattern_ref, factor_ref, pair):
        for block in range(half):
            columns = slice(block * width, (block + 1) * width)
            kept = jnp.broadcast_to(pattern_ref[pair][:, block : block + 1].astype(f32), (width, width))
            out_ref[place, :, columns] = factor_ref[pair, :, columns] * kept.astype(bf16)

    def first_mask(factor_hbm, pattern_hbm, masked_ref, pattern_out, factor_ref, pattern_ref, sems):
        order = groups[0]
        small = [pltpu.make_async_copy(pattern_hbm, pattern_ref, sems.at[0])]
        large = [
            pltpu.make_async_copy(factor_hbm.at[pair], factor_ref.at[pair], sems.at[1 + k])
            for k, pair in enumerate(order)
        ]
        for copy in small + large:
            copy.start()
        for copy in small:
            copy.wait()
        pattern_out[...] = pattern_ref[...]
        for copy, pair in zip(large, order):
            copy.wait()
            group, place = place_of[pair]
            mask_pair(masked_ref, place, pattern_ref, factor_ref, pair)

    def first(
        rhs_hbm, factor_hbm, pattern_ref, widths_hbm, inverse_hbm,
        solved_ref, out_ref, rhs_ref, solver_ref, *refs,
    ):
        masked_refs = [None, *refs[: len(groups) - 1]]
        factor_ref, inverse_ref, widths_ref, sems = refs[len(groups) - 1 :]
        later = needed[len(groups[0]) :]
        small = [
            pltpu.make_async_copy(widths_hbm, widths_ref, sems.at[0]),
            pltpu.make_async_copy(rhs_hbm, rhs_ref, sems.at[1]),
            pltpu.make_async_copy(inverse_hbm, inverse_ref, sems.at[2]),
        ]
        large = [
            pltpu.make_async_copy(factor_hbm.at[pair], factor_ref.at[pair], sems.at[3 + k])
            for k, pair in enumerate(later)
        ]
        for copy in small + large:
            copy.start()
        for copy in small:
            copy.wait()
        row = lax.broadcasted_iota(jnp.int32, (width, width), 0)
        column = lax.broadcasted_iota(jnp.int32, (width, width), 1)
        for level in range(levels):
            live = jnp.broadcast_to(widths_ref[:, level : level + 1], (width, width))
            inverse = jnp.where((row < live) & (column < live), inverse_ref[level], 0.0)
            if level == 0:
                value = lax.dot_general(
                    rhs_ref[0], inverse, (((1,), (1,)), ((), ())), precision=HIGHEST, preferred_element_type=f32
                )
                solved_ref[...] = value
                spread(out_ref, value)
            if level in forward_slot:
                store_solver(solver_ref, forward_slot[level], inverse.T)
            if level in backward_slot:
                store_solver(solver_ref, backward_slot[level], inverse)
            if level == levels - 1:
                both = lax.dot_general(
                    inverse, inverse, (((0,), (0,)), ((), ())), precision=HIGHEST, preferred_element_type=f32
                )
                store_solver(solver_ref, top_slot, both)
        for copy, pair in zip(large, later):
            copy.wait()
            group, place = place_of[pair]
            mask_pair(masked_refs[group], place, pattern_ref, factor_ref, pair)

    def flat(held):
        return [m for moved in held for m in moved]

    def matrix(refs, level, lower, shift):
        group, place = place_of[lookup[level, lower]]
        return refs[group * col_parts + shift][place]

    def middle(level):
        def body(rhs_ref, solver_ref, *refs):
            gathered, matrices = refs[:level], refs[level:-2]
            solved_ref, out_ref = refs[-2:]
            total = forward_total(gathered, level, matrices)
            value = solve(solver_ref, forward_slot[level], rhs_ref[level] - total)
            solved_ref[...] = value
            spread(out_ref, value)

        return body

    def top(rhs_ref, solver_ref, *refs):
        level = levels - 1
        gathered, matrices = refs[:level], refs[level:-4]
        result_ref, rounded_ref, keep_ref, give_ref = refs[-4:]
        total = forward_total(gathered, level, matrices)
        result = solve(solver_ref, top_slot, rhs_ref[level] - total)
        result_ref[...] = result
        rounded = result.astype(bf16)
        rounded_ref[...] = rounded
        backward_partials(keep_ref, give_ref, {level: rounded}, level - 1, matrices)

    def backward_early(lower):
        known = range(lower + 2, levels)

        def body(*refs):
            solved = {level: refs[k][...] for k, level in enumerate(known)}
            matrices, (keep_ref, give_ref) = refs[len(known) : -2], refs[-2:]
            backward_partials(keep_ref, give_ref, solved, lower, matrices)

        return body

    def down(level):
        def body(solver_ref, solved_ref, sums_ref, early_keep_ref, early_give_ref, *refs):
            outs = 3 + (level > 1)
            matrices = refs[:-outs]
            keep_ref, give_ref, result_ref = refs[-outs:][:3]
            corrected = solved_ref[...] - jnp.sum(sums_ref[...], axis=0)
            result = solve(solver_ref, backward_slot[level], corrected)
            result_ref[...] = result
            rounded = result.astype(bf16)
            if level > 1:
                refs[-1][...] = rounded
            begun = early_keep_ref, early_give_ref
            backward_partials(keep_ref, give_ref, {level: rounded}, level - 1, matrices, begun)

        return body

    def last(solver_ref, solved_ref, sums_ref, *refs):
        out_ref = refs[-1]
        corrected = solved_ref[...] - jnp.sum(sums_ref[...], axis=0)
        out_ref[0] = solve(solver_ref, backward_slot[0], corrected)
        for level in range(1, levels):
            out_ref[level] = refs[level - 1][...]

    def exchange(own):
        shifted = [own]
        for shift in range(1, col_parts):
            to_lower = [((q + shift) % col_parts, q) for q in range(col_parts)]
            shifted.append(lax.ppermute(own, "col", to_lower))
        return shifted

    def trade_beside(blocks, group):
        moved = exchange(masked[group]) if group < len(groups) else None
        blocks = trade(blocks)
        for later in range(group + 1, len(groups)):
            masked[later], blocks = lax.optimization_barrier((masked[later], blocks))
        return blocks, moved

    solved, gathered, held = [], [], []
    with jax.named_scope("forward_first"):
        operands = [
            pltpu.with_memory_space_constraint(x, pltpu.HBM)
            for x in (right_sides, factors, pattern, live_widths.reshape(1, levels), inverses)
        ]
        masked0, pattern_vmem = call(first_mask,
            (jax.ShapeDtypeStruct((len(groups[0]), width, local_cols), bf16), jax.ShapeDtypeStruct(pattern.shape, jnp.int32)),
            operands[1], operands[2], space=pltpu.HBM,
            scratch=[
                pltpu.VMEM(factors.shape, bf16),
                pltpu.VMEM(pattern.shape, jnp.int32),
                pltpu.SemaphoreType.DMA((1 + pairs,)),
            ],
        )
        operands[2] = pattern_vmem
        value, out, right_sides, solver, *masked = call(
            first,
            (block_f32, spread_bf16, shaped(levels, rhs, width), jax.ShapeDtypeStruct((slots, deep, width), bf16))
            + tuple(jax.ShapeDtypeStruct((len(group), width, local_cols), bf16) for group in groups[1:]),
            *operands,
            spaces=[pltpu.HBM, pltpu.HBM, pltpu.VMEM, pltpu.HBM, pltpu.HBM],
            scratch=[
                pltpu.VMEM(factors.shape, bf16),
                pltpu.VMEM(inverses.shape, f32),
                pltpu.VMEM((1, levels), jnp.int32),
                pltpu.SemaphoreType.DMA((3 + pairs,)),
            ],
        )
        masked = [masked0, *masked]
    solved.append(value)
    blocks, moved = trade_beside(out, 0)
    gathered.append(blocks)
    held.append(moved)
    for level in range(1, levels - 1):
        with jax.named_scope("forward_level"):
            value, out = call(middle(level), (block_f32, spread_bf16), right_sides, solver, *gathered, *flat(held))
        solved.append(value)
        blocks, moved = trade_beside(out, level)
        gathered.append(blocks)
        if moved is not None:
            held.append(moved)
    factors = flat(held)
    results, rounded = {}, {}
    level = levels - 1
    with jax.named_scope("top_level"):
        results[level], rounded[level], *halves = call(
            top, (block_f32, block_bf16, twins_f32, twins_f32), right_sides, solver, *gathered, *factors
        )

    def begin(lower):
        with jax.named_scope("backward_early"):
            known = [rounded[level] for level in range(lower + 2, levels)]
            return call(backward_early(lower), (twins_f32, twins_f32), *known, *factors)

    for level in range(levels - 2, 0, -1):
        sums, begun = scatter(*halves, lambda: begin(level - 1))
        with jax.named_scope("backward_level"):
            keep, give, results[level], *rest = call(
                down(level),
                (twins_f32, twins_f32, block_f32) + (block_bf16,) * (level > 1),
                solver,
                solved[level],
                sums,
                *begun,
                *factors,
            )
        halves = keep, give
        rounded[level] = rest[0] if rest else None
    sums, _ = scatter(*halves)
    with jax.named_scope("backward_last"):
        return call(
            last,
            jax.ShapeDtypeStruct((levels, rhs, width), f32),
            solver,
            solved[0],
            sums,
            *[results[level] for level in range(1, levels)],
        )


def solution(mesh):
    parts = (mesh.shape["row"], mesh.shape["col"])

    def run(*operands):
        return local(parts, *operands)

    return jax.shard_map(
        run,
        mesh=mesh,
        in_specs=(
            P(None, "col", "row"),
            P(None, "row", "col"),
            P(None, "row", "col"),
            P(None, "row"),
            P(None, "row", None, None),
        ),
        out_specs=P(None, "col", "row"),
        check_vma=False,
    )
```

```python
import math

import jax
import jax.numpy as jnp
from jax import lax
from jax.experimental import pallas as pl
from jax.experimental.pallas import tpu as pltpu
from jax.sharding import PartitionSpec as P

HIGHEST = lax.Precision.HIGHEST


def pair_lookup(level_count):
    lookup = {}
    for lower_level in range(level_count):
        for above_level in range(lower_level + 1, level_count):
            lookup[above_level, lower_level] = len(lookup)
    return lookup


def call(kernel, outs, *operands, space=pltpu.VMEM, spaces=None, scratch=()):
    return pl.pallas_call(
        kernel,
        out_shape=outs,
        in_specs=[pl.BlockSpec(memory_space=s) for s in (spaces or [space] * len(operands))],
        out_specs=jax.tree.map(lambda _: pl.BlockSpec(memory_space=pltpu.VMEM), outs),
        scratch_shapes=scratch,
        compiler_params=pltpu.CompilerParams(vmem_limit_bytes=48 * 1024 * 1024),
    )(*operands)


def local(parts, right_sides, factors, pattern, live_widths, inverses):
    row_parts, col_parts = parts
    levels, rhs, width = right_sides.shape
    pairs, _, local_cols = factors.shape
    half = local_cols // width
    total_blocks = half * col_parts
    lookup = pair_lookup(levels)
    needed = [lookup[level, lower] for level in range(1, levels) for lower in range(level)]
    group_size = -(-pairs // (levels - 1))
    groups = [needed[k : k + group_size] for k in range(0, pairs, group_size)]
    place_of = {pair: (g, k) for g, group in enumerate(groups) for k, pair in enumerate(group)}
    inverses = inverses.reshape(levels, width, width)
    f32, bf16 = jnp.float32, jnp.bfloat16

    def shaped(*shape):
        return jax.ShapeDtypeStruct(shape, f32)

    block_f32 = jax.ShapeDtypeStruct((rhs, width), f32)
    block_bf16 = jax.ShapeDtypeStruct((rhs, width), bf16)
    spread_bf16 = jax.ShapeDtypeStruct((total_blocks, rhs, width), bf16)
    twins = row_parts // 2
    twins_f32 = jax.ShapeDtypeStruct((twins, rhs, width), f32)

    middle_row = 2 * (twins // 2 + 1) + 1
    row_order = [middle_row] + [k for k in range(0, row_parts, 2)] + [k for k in range(1, row_parts, 2) if k != middle_row]
    step = next(s for s in range(5, 5 + twins) if math.gcd(s, twins) == 1)
    twin_orders = [[(root + step * k) % twins for k in range(twins)] for root in (twins // 2, twins // 2 + 1)]

    def row_place(index):
        odd_place = twins + index // 2 + jnp.where(index < middle_row, 1, 0)
        odd_place = jnp.where(index == middle_row, 0, odd_place)
        return jnp.where(lax.rem(index, 2) == 0, 1 + index // 2, odd_place)

    def trade(blocks):
        return lax.all_to_all(blocks, "row", 0, 0, axis_index_groups=[row_order])

    def scatter(keep, give, early=None):
        taken = lax.ppermute(give, "row", [(k, k ^ 1) for k in range(row_parts)])
        begun = early() if early else ()
        with jax.named_scope("sum_twins"):
            sums = call(add, twins_f32, keep, taken)
        sums, begun = lax.optimization_barrier((sums, begun))
        one_of_each = [[2 * g + (g + side) % 2 for g in order] for side, order in zip((1, 0), twin_orders)]
        return lax.all_to_all(sums, "row", 0, 0, axis_index_groups=one_of_each), begun

    left_parts, right_parts = (0, 0, 1, 0, 1, 2), (0, 1, 0, 2, 1, 0)
    deep = len(left_parts) * width
    forward_slot = {level: level - 1 for level in range(1, levels - 1)}
    top_slot = levels - 2
    backward_slot = {level: levels - 1 + level for level in range(levels - 1)}
    slots = 2 * levels - 2

    def split(value):
        parts = []
        for _ in range(3):
            parts.append(value.astype(bf16))
            value = value - parts[-1].astype(f32)
        return parts

    def store_solver(solver_ref, slot, matrix):
        parts = split(matrix)
        for k, part in enumerate(right_parts):
            solver_ref[slot, k * width : (k + 1) * width, :] = parts[part]

    def solve(solver_ref, slot, vector):
        parts = split(vector)
        left = jnp.concatenate([parts[part] for part in left_parts], axis=1)
        return lax.dot_general(left, solver_ref[slot], (((1,), (0,)), ((), ())), preferred_element_type=f32)

    def forward_total(gathered, level, matrices, late=None, total=None):
        mine = lax.axis_index("col")
        for shift in range(col_parts):
            start = lax.rem(mine + shift, col_parts) * half
            for lower in range(level):
                is_late = shift > 0 and place_of[lookup[level, lower]][0] == len(groups) - 1
                if late is not None and is_late != late:
                    continue
                left = jnp.concatenate([gathered[lower][row_place(start + k)] for k in range(half)], axis=1)
                term = lax.dot_general(
                    left, matrix(matrices, level, lower, shift), (((1,), (1,)), ((), ())), preferred_element_type=f32
                )
                total = term if total is None else total + term
        return total

    def add(left_ref, right_ref, out_ref):
        index = lax.axis_index("row")
        second = lax.rem(index + index // 2, 2) == 0
        for place in range(twins):
            g = jnp.where(second, twin_orders[1][place], twin_orders[0][place])
            out_ref[place] = left_ref[g] + right_ref[g]

    def backward_partials(keep_ref, give_ref, solved, lower, matrices, begun=None):
        mine = lax.axis_index("col")
        index = lax.axis_index("row")
        for shift in range(col_parts):
            start = lax.rem(mine + shift, col_parts) * half
            total = None
            for level, vector in solved.items():
                term = lax.dot_general(
                    vector, matrix(matrices, level, lower, shift), (((1,), (0,)), ((), ())), preferred_element_type=f32
                )
                total = term if total is None else total + term
            for block in range(0, half, 2):
                even = total[:, block * width : (block + 1) * width]
                uneven = total[:, (block + 1) * width : (block + 2) * width]
                g = start // 2 + block // 2
                kept, given = (0.0, 0.0) if begun is None else (begun[0][g], begun[1][g])
                odd = lax.rem(index + index // 2 + g, 2) == 1
                keep_ref[g] = jnp.where(odd, uneven, even) + kept
                give_ref[g] = jnp.where(odd, even, uneven) + given

    def spread(out_ref, value):
        out_ref[...] = jnp.broadcast_to(value.astype(bf16)[None], out_ref.shape)

    def mask_pair(out_ref, place, pattern_ref, factor_ref, pair):
        for block in range(half):
            columns = slice(block * width, (block + 1) * width)
            kept = jnp.broadcast_to(pattern_ref[pair][:, block : block + 1].astype(f32), (width, width))
            out_ref[place, :, columns] = factor_ref[pair, :, columns] * kept.astype(bf16)

    def first_mask(factor_hbm, pattern_hbm, masked_ref, pattern_out, factor_ref, pattern_ref, sems):
        order = groups[0]
        small = [pltpu.make_async_copy(pattern_hbm, pattern_ref, sems.at[0])]
        large = [
            pltpu.make_async_copy(factor_hbm.at[pair], factor_ref.at[pair], sems.at[1 + k])
            for k, pair in enumerate(order)
        ]
        for copy in small + large:
            copy.start()
        for copy in small:
            copy.wait()
        pattern_out[...] = pattern_ref[...]
        for copy, pair in zip(large, order):
            copy.wait()
            group, place = place_of[pair]
            mask_pair(masked_ref, place, pattern_ref, factor_ref, pair)

    def first(
        rhs_hbm, factor_hbm, pattern_ref, widths_hbm, inverse_hbm,
        solved_ref, out_ref, rhs_ref, solver_ref, *refs,
    ):
        masked_refs = [None, *refs[: len(groups) - 1]]
        factor_ref, inverse_ref, widths_ref, sems = refs[len(groups) - 1 :]
        later = needed[len(groups[0]) :]
        small = [
            pltpu.make_async_copy(widths_hbm, widths_ref, sems.at[0]),
            pltpu.make_async_copy(rhs_hbm, rhs_ref, sems.at[1]),
            pltpu.make_async_copy(inverse_hbm, inverse_ref, sems.at[2]),
        ]
        large = [
            pltpu.make_async_copy(factor_hbm.at[pair], factor_ref.at[pair], sems.at[3 + k])
            for k, pair in enumerate(later)
        ]
        for copy in small + large:
            copy.start()
        for copy in small:
            copy.wait()
        row = lax.broadcasted_iota(jnp.int32, (width, width), 0)
        column = lax.broadcasted_iota(jnp.int32, (width, width), 1)
        for level in range(levels):
            live = jnp.broadcast_to(widths_ref[:, level : level + 1], (width, width))
            inverse = jnp.where((row < live) & (column < live), inverse_ref[level], 0.0)
            if level == 0:
                value = lax.dot_general(
                    rhs_ref[0], inverse, (((1,), (1,)), ((), ())), precision=HIGHEST, preferred_element_type=f32
                )
                solved_ref[...] = value
                spread(out_ref, value)
            if level in forward_slot:
                store_solver(solver_ref, forward_slot[level], inverse.T)
            if level in backward_slot:
                store_solver(solver_ref, backward_slot[level], inverse)
            if level == levels - 1:
                both = lax.dot_general(
                    inverse, inverse, (((0,), (0,)), ((), ())), precision=HIGHEST, preferred_element_type=f32
                )
                store_solver(solver_ref, top_slot, both)
        for copy, pair in zip(large, later):
            copy.wait()
            group, place = place_of[pair]
            mask_pair(masked_refs[group], place, pattern_ref, factor_ref, pair)

    def flat(held):
        return [m for moved in held for m in moved]

    def matrix(refs, level, lower, shift):
        group, place = place_of[lookup[level, lower]]
        return refs[group * col_parts + shift][place]

    def middle(level):
        def body(rhs_ref, solver_ref, *refs):
            gathered, matrices = refs[:level], refs[level:-2]
            solved_ref, out_ref = refs[-2:]
            total = forward_total(gathered, level, matrices)
            value = solve(solver_ref, forward_slot[level], rhs_ref[level] - total)
            solved_ref[...] = value
            spread(out_ref, value)

        return body

    def top_early(*refs):
        level = levels - 1
        refs[-1][...] = forward_total(refs[:level], level, refs[level:-1], False)

    def top(rhs_ref, solver_ref, early_ref, *refs):
        level = levels - 1
        gathered, matrices = refs[:level], refs[level:-4]
        result_ref, rounded_ref, keep_ref, give_ref = refs[-4:]
        total = forward_total(gathered, level, matrices, True, early_ref[...])
        result = solve(solver_ref, top_slot, rhs_ref[level] - total)
        result_ref[...] = result
        rounded = result.astype(bf16)
        rounded_ref[...] = rounded
        backward_partials(keep_ref, give_ref, {level: rounded}, level - 1, matrices)

    def backward_early(lower):
        known = range(lower + 2, levels)

        def body(*refs):
            solved = {level: refs[k][...] for k, level in enumerate(known)}
            matrices, (keep_ref, give_ref) = refs[len(known) : -2], refs[-2:]
            backward_partials(keep_ref, give_ref, solved, lower, matrices)

        return body

    def down(level):
        def body(solver_ref, solved_ref, sums_ref, early_keep_ref, early_give_ref, *refs):
            outs = 3 + (level > 1)
            matrices = refs[:-outs]
            keep_ref, give_ref, result_ref = refs[-outs:][:3]
            corrected = solved_ref[...] - jnp.sum(sums_ref[...], axis=0)
            result = solve(solver_ref, backward_slot[level], corrected)
            result_ref[...] = result
            rounded = result.astype(bf16)
            if level > 1:
                refs[-1][...] = rounded
            begun = early_keep_ref, early_give_ref
            backward_partials(keep_ref, give_ref, {level: rounded}, level - 1, matrices, begun)

        return body

    def last(solver_ref, solved_ref, sums_ref, *refs):
        out_ref = refs[-1]
        corrected = solved_ref[...] - jnp.sum(sums_ref[...], axis=0)
        out_ref[0] = solve(solver_ref, backward_slot[0], corrected)
        for level in range(1, levels):
            out_ref[level] = refs[level - 1][...]

    def exchange(own):
        shifted = [own]
        for shift in range(1, col_parts):
            to_lower = [((q + shift) % col_parts, q) for q in range(col_parts)]
            shifted.append(lax.ppermute(own, "col", to_lower))
        return shifted

    def trade_beside(blocks, group):
        moved = exchange(masked[group]) if group < len(groups) else None
        blocks = trade(blocks)
        for later in range(group + 1, len(groups)):
            masked[later], blocks = lax.optimization_barrier((masked[later], blocks))
        return blocks, moved

    solved, gathered, held = [], [], []
    with jax.named_scope("forward_first"):
        operands = [
            pltpu.with_memory_space_constraint(x, pltpu.HBM)
            for x in (right_sides, factors, pattern, live_widths.reshape(1, levels), inverses)
        ]
        masked0, pattern_vmem = call(
            first_mask,
            (jax.ShapeDtypeStruct((len(groups[0]), width, local_cols), bf16), jax.ShapeDtypeStruct(pattern.shape, jnp.int32)),
            operands[1], operands[2], space=pltpu.HBM,
            scratch=[
                pltpu.VMEM(factors.shape, bf16),
                pltpu.VMEM(pattern.shape, jnp.int32),
                pltpu.SemaphoreType.DMA((1 + pairs,)),
            ],
        )
        operands[2] = pattern_vmem
        value, out, right_sides, solver, *masked = call(
            first,
            (block_f32, spread_bf16, shaped(levels, rhs, width), jax.ShapeDtypeStruct((slots, deep, width), bf16))
            + tuple(jax.ShapeDtypeStruct((len(group), width, local_cols), bf16) for group in groups[1:]),
            *operands,
            spaces=[pltpu.HBM, pltpu.HBM, pltpu.VMEM, pltpu.HBM, pltpu.HBM],
            scratch=[
                pltpu.VMEM(factors.shape, bf16),
                pltpu.VMEM(inverses.shape, f32),
                pltpu.VMEM((1, levels), jnp.int32),
                pltpu.SemaphoreType.DMA((3 + pairs,)),
            ],
        )
        masked = [masked0, *masked]
    solved.append(value)
    blocks, moved = trade_beside(out, 0)
    gathered.append(blocks)
    held.append(moved)
    for level in range(1, levels - 1):
        with jax.named_scope("forward_level"):
            value, out = call(middle(level), (block_f32, spread_bf16), right_sides, solver, *gathered, *flat(held))
        solved.append(value)
        blocks, moved = trade_beside(out, level)
        gathered.append(blocks)
        if moved is not None:
            held.append(moved)
    factors = flat(held)
    results, rounded = {}, {}
    level = levels - 1
    with jax.named_scope("top_early"):
        arrived = factors[: len(factors) - (col_parts - 1)]
        early = call(top_early, block_f32, *gathered, *arrived)
    with jax.named_scope("top_level"):
        results[level], rounded[level], *halves = call(
            top, (block_f32, block_bf16, twins_f32, twins_f32), right_sides, solver, early, *gathered, *factors
        )

    def begin(lower):
        with jax.named_scope("backward_early"):
            known = [rounded[level] for level in range(lower + 2, levels)]
            return call(backward_early(lower), (twins_f32, twins_f32), *known, *factors)

    for level in range(levels - 2, 0, -1):
        sums, begun = scatter(*halves, lambda: begin(level - 1))
        with jax.named_scope("backward_level"):
            keep, give, results[level], *rest = call(
                down(level),
                (twins_f32, twins_f32, block_f32) + (block_bf16,) * (level > 1),
                solver,
                solved[level],
                sums,
                *begun,
                *factors,
            )
        halves = keep, give
        rounded[level] = rest[0] if rest else None
    sums, _ = scatter(*halves)
    with jax.named_scope("backward_last"):
        return call(
            last,
            jax.ShapeDtypeStruct((levels, rhs, width), f32),
            solver,
            solved[0],
            sums,
            *[results[level] for level in range(1, levels)],
        )


def solution(mesh):
    parts = (mesh.shape["row"], mesh.shape["col"])

    def run(*operands):
        return local(parts, *operands)

    return jax.shard_map(
        run,
        mesh=mesh,
        in_specs=(
            P(None, "col", "row"),
            P(None, "row", "col"),
            P(None, "row", "col"),
            P(None, "row"),
            P(None, "row", None, None),
        ),
        out_specs=P(None, "col", "row"),
        check_vma=False,
    )
```

```python
import math

import jax
import jax.numpy as jnp
from jax import lax
from jax.experimental import pallas as pl
from jax.experimental.pallas import tpu as pltpu
from jax.sharding import PartitionSpec as P

HIGHEST = lax.Precision.HIGHEST


def pair_lookup(level_count):
    lookup = {}
    for lower_level in range(level_count):
        for above_level in range(lower_level + 1, level_count):
            lookup[above_level, lower_level] = len(lookup)
    return lookup


def call(kernel, outs, *operands, space=pltpu.VMEM, spaces=None, scratch=()):
    return pl.pallas_call(
        kernel,
        out_shape=outs,
        in_specs=[pl.BlockSpec(memory_space=s) for s in (spaces or [space] * len(operands))],
        out_specs=jax.tree.map(lambda _: pl.BlockSpec(memory_space=pltpu.VMEM), outs),
        scratch_shapes=scratch,
        compiler_params=pltpu.CompilerParams(vmem_limit_bytes=48 * 1024 * 1024),
    )(*operands)


def local(parts, right_sides, factors, pattern, live_widths, inverses):
    row_parts, col_parts = parts
    levels, rhs, width = right_sides.shape
    pairs, _, local_cols = factors.shape
    half = local_cols // width
    total_blocks = half * col_parts
    lookup = pair_lookup(levels)
    needed = [lookup[level, lower] for level in range(1, levels) for lower in range(level)]
    group_size = -(-pairs // (levels - 1))
    groups = [needed[k : k + group_size] for k in range(0, pairs, group_size)]
    place_of = {pair: (g, k) for g, group in enumerate(groups) for k, pair in enumerate(group)}
    inverses = inverses.reshape(levels, width, width)
    f32, bf16 = jnp.float32, jnp.bfloat16

    def shaped(*shape):
        return jax.ShapeDtypeStruct(shape, f32)

    block_f32 = jax.ShapeDtypeStruct((rhs, width), f32)
    block_bf16 = jax.ShapeDtypeStruct((rhs, width), bf16)
    spread_bf16 = jax.ShapeDtypeStruct((total_blocks, rhs, width), bf16)
    twins = row_parts // 2
    twins_f32 = jax.ShapeDtypeStruct((twins, rhs, width), f32)

    middle_row = 2 * (twins // 2 + 1) + 1
    row_order = [middle_row] + [k for k in range(0, row_parts, 2)] + [k for k in range(1, row_parts, 2) if k != middle_row]
    step = next(s for s in range(5, 5 + twins) if math.gcd(s, twins) == 1)
    twin_orders = [[(root + step * k) % twins for k in range(twins)] for root in (twins // 2, twins // 2 + 1)]

    def row_place(index):
        odd_place = twins + index // 2 + jnp.where(index < middle_row, 1, 0)
        odd_place = jnp.where(index == middle_row, 0, odd_place)
        return jnp.where(lax.rem(index, 2) == 0, 1 + index // 2, odd_place)

    def trade(blocks):
        return lax.all_to_all(blocks, "row", 0, 0, axis_index_groups=[row_order])

    def scatter(begin_keep, give, early=None):
        taken = lax.ppermute(give, "row", [(k, k ^ 1) for k in range(row_parts)])
        keep = begin_keep()
        begun = early() if early else ()
        with jax.named_scope("sum_twins"):
            sums = call(add, twins_f32, keep, taken)
        sums, begun = lax.optimization_barrier((sums, begun))
        one_of_each = [[2 * g + (g + side) % 2 for g in order] for side, order in zip((1, 0), twin_orders)]
        return lax.all_to_all(sums, "row", 0, 0, axis_index_groups=one_of_each), begun

    left_parts, right_parts = (0, 0, 1, 0, 1, 2), (0, 1, 0, 2, 1, 0)
    deep = len(left_parts) * width
    forward_slot = {level: level - 1 for level in range(1, levels - 1)}
    top_slot = levels - 2
    backward_slot = {level: levels - 1 + level for level in range(levels - 1)}
    slots = 2 * levels - 2

    def split(value):
        parts = []
        for _ in range(3):
            parts.append(value.astype(bf16))
            value = value - parts[-1].astype(f32)
        return parts

    def store_solver(solver_ref, slot, matrix):
        parts = split(matrix)
        for k, part in enumerate(right_parts):
            solver_ref[slot, k * width : (k + 1) * width, :] = parts[part]

    def solve(solver_ref, slot, vector):
        parts = split(vector)
        left = jnp.concatenate([parts[part] for part in left_parts], axis=1)
        return lax.dot_general(left, solver_ref[slot], (((1,), (0,)), ((), ())), preferred_element_type=f32)

    def forward_total(gathered, level, matrices, late=None, total=None):
        mine = lax.axis_index("col")
        for shift in range(col_parts):
            start = lax.rem(mine + shift, col_parts) * half
            for lower in range(level):
                is_late = shift > 0 and place_of[lookup[level, lower]][0] == len(groups) - 1
                if late is not None and is_late != late:
                    continue
                left = jnp.concatenate([gathered[lower][row_place(start + k)] for k in range(half)], axis=1)
                term = lax.dot_general(
                    left, matrix(matrices, level, lower, shift), (((1,), (1,)), ((), ())), preferred_element_type=f32
                )
                total = term if total is None else total + term
        return total

    def add(left_ref, right_ref, out_ref):
        index = lax.axis_index("row")
        second = lax.rem(index + index // 2, 2) == 0
        for place in range(twins):
            g = jnp.where(second, twin_orders[1][place], twin_orders[0][place])
            out_ref[place] = left_ref[g] + right_ref[g]

    def backward_partials(out_ref, solved, lower, matrices, begun, give):
        mine = lax.axis_index("col")
        index = lax.axis_index("row")
        for shift in range(col_parts):
            start = lax.rem(mine + shift, col_parts) * half
            pairs_of = [(start // 2 + k, 2 * k) for k in range(half // 2)]
            offsets = []
            for g, block in pairs_of:
                odd = lax.rem(index + index // 2 + g, 2)
                chosen = block + (1 - odd if give else odd)
                offsets.append(pl.multiple_of(chosen * width, width))
            total = None
            for level, vector in solved.items():
                group, place = place_of[lookup[level, lower]]
                ref = matrices[group * col_parts + shift]
                right = jnp.concatenate([ref[place, :, pl.ds(offset, width)] for offset in offsets], axis=1)
                term = lax.dot_general(vector, right, (((1,), (0,)), ((), ())), preferred_element_type=f32)
                total = term if total is None else total + term
            for k, (g, _) in enumerate(pairs_of):
                block = total[:, k * width : (k + 1) * width]
                out_ref[g] = block if begun is None else block + begun[g]

    def keep_partials(level):
        def body(rounded_ref, *refs):
            begun, matrices = (refs[0], refs[1:-1]) if level < levels - 1 else (None, refs[:-1])
            backward_partials(refs[-1], {level: rounded_ref[...]}, level - 1, matrices, begun, False)

        return body

    def spread(out_ref, value):
        out_ref[...] = jnp.broadcast_to(value.astype(bf16)[None], out_ref.shape)

    def mask_pair(out_ref, place, pattern_ref, factor_ref, pair):
        for block in range(half):
            columns = slice(block * width, (block + 1) * width)
            kept = jnp.broadcast_to(pattern_ref[pair][:, block : block + 1].astype(f32), (width, width))
            out_ref[place, :, columns] = factor_ref[pair, :, columns] * kept.astype(bf16)

    def first_mask(factor_hbm, pattern_hbm, masked_ref, pattern_out, factor_ref, pattern_ref, sems):
        order = groups[0]
        small = [pltpu.make_async_copy(pattern_hbm, pattern_ref, sems.at[0])]
        large = [
            pltpu.make_async_copy(factor_hbm.at[pair], factor_ref.at[pair], sems.at[1 + k])
            for k, pair in enumerate(order)
        ]
        for copy in small + large:
            copy.start()
        for copy in small:
            copy.wait()
        pattern_out[...] = pattern_ref[...]
        for copy, pair in zip(large, order):
            copy.wait()
            group, place = place_of[pair]
            mask_pair(masked_ref, place, pattern_ref, factor_ref, pair)

    def first(
        rhs_hbm, factor_hbm, pattern_ref, widths_hbm, inverse_hbm,
        solved_ref, out_ref, rhs_ref, solver_ref, *refs,
    ):
        masked_refs = [None, *refs[: len(groups) - 1]]
        factor_ref, inverse_ref, widths_ref, sems = refs[len(groups) - 1 :]
        later = needed[len(groups[0]) :]
        small = [
            pltpu.make_async_copy(widths_hbm, widths_ref, sems.at[0]),
            pltpu.make_async_copy(rhs_hbm, rhs_ref, sems.at[1]),
            pltpu.make_async_copy(inverse_hbm, inverse_ref, sems.at[2]),
        ]
        large = [
            pltpu.make_async_copy(factor_hbm.at[pair], factor_ref.at[pair], sems.at[3 + k])
            for k, pair in enumerate(later)
        ]
        for copy in small + large:
            copy.start()
        for copy in small:
            copy.wait()
        row = lax.broadcasted_iota(jnp.int32, (width, width), 0)
        column = lax.broadcasted_iota(jnp.int32, (width, width), 1)
        for level in range(levels):
            live = jnp.broadcast_to(widths_ref[:, level : level + 1], (width, width))
            inverse = jnp.where((row < live) & (column < live), inverse_ref[level], 0.0)
            if level == 0:
                value = lax.dot_general(
                    rhs_ref[0], inverse, (((1,), (1,)), ((), ())), precision=HIGHEST, preferred_element_type=f32
                )
                solved_ref[...] = value
                spread(out_ref, value)
            if level in forward_slot:
                store_solver(solver_ref, forward_slot[level], inverse.T)
            if level in backward_slot:
                store_solver(solver_ref, backward_slot[level], inverse)
            if level == levels - 1:
                both = lax.dot_general(
                    inverse, inverse, (((0,), (0,)), ((), ())), precision=HIGHEST, preferred_element_type=f32
                )
                store_solver(solver_ref, top_slot, both)
        for copy, pair in zip(large, later):
            copy.wait()
            group, place = place_of[pair]
            mask_pair(masked_refs[group], place, pattern_ref, factor_ref, pair)

    def flat(held):
        return [m for moved in held for m in moved]

    def matrix(refs, level, lower, shift):
        group, place = place_of[lookup[level, lower]]
        return refs[group * col_parts + shift][place]

    def middle(level):
        def body(rhs_ref, solver_ref, *refs):
            gathered, matrices = refs[:level], refs[level:-2]
            solved_ref, out_ref = refs[-2:]
            total = forward_total(gathered, level, matrices)
            value = solve(solver_ref, forward_slot[level], rhs_ref[level] - total)
            solved_ref[...] = value
            spread(out_ref, value)

        return body

    def top_early(*refs):
        level = levels - 1
        refs[-1][...] = forward_total(refs[:level], level, refs[level:-1], False)

    def top(rhs_ref, solver_ref, early_ref, *refs):
        level = levels - 1
        gathered, matrices = refs[:level], refs[level:-3]
        result_ref, rounded_ref, give_ref = refs[-3:]
        total = forward_total(gathered, level, matrices, True, early_ref[...])
        result = solve(solver_ref, top_slot, rhs_ref[level] - total)
        result_ref[...] = result
        rounded = result.astype(bf16)
        rounded_ref[...] = rounded
        backward_partials(give_ref, {level: rounded}, level - 1, matrices, None, True)

    def backward_early(lower):
        known = range(lower + 2, levels)

        def body(*refs):
            solved = {level: refs[k][...] for k, level in enumerate(known)}
            matrices, (keep_ref, give_ref) = refs[len(known) : -2], refs[-2:]
            backward_partials(keep_ref, solved, lower, matrices, None, False)
            backward_partials(give_ref, solved, lower, matrices, None, True)

        return body

    def down(level):
        def body(solver_ref, solved_ref, sums_ref, early_give_ref, *refs):
            matrices = refs[:-3]
            give_ref, result_ref, rounded_ref = refs[-3:]
            corrected = solved_ref[...] - jnp.sum(sums_ref[...], axis=0)
            result = solve(solver_ref, backward_slot[level], corrected)
            result_ref[...] = result
            rounded = result.astype(bf16)
            rounded_ref[...] = rounded
            backward_partials(give_ref, {level: rounded}, level - 1, matrices, early_give_ref, True)

        return body

    def last(solver_ref, solved_ref, sums_ref, *refs):
        out_ref = refs[-1]
        corrected = solved_ref[...] - jnp.sum(sums_ref[...], axis=0)
        out_ref[0] = solve(solver_ref, backward_slot[0], corrected)
        for level in range(1, levels):
            out_ref[level] = refs[level - 1][...]

    def exchange(own):
        shifted = [own]
        for shift in range(1, col_parts):
            to_lower = [((q + shift) % col_parts, q) for q in range(col_parts)]
            shifted.append(lax.ppermute(own, "col", to_lower))
        return shifted

    def trade_beside(blocks, group):
        moved = exchange(masked[group]) if group < len(groups) else None
        blocks = trade(blocks)
        for later in range(group + 1, len(groups)):
            masked[later], blocks = lax.optimization_barrier((masked[later], blocks))
        return blocks, moved

    solved, gathered, held = [], [], []
    with jax.named_scope("forward_first"):
        operands = [
            pltpu.with_memory_space_constraint(x, pltpu.HBM)
            for x in (right_sides, factors, pattern, live_widths.reshape(1, levels), inverses)
        ]
        masked0, pattern_vmem = call(
            first_mask,
            (jax.ShapeDtypeStruct((len(groups[0]), width, local_cols), bf16), jax.ShapeDtypeStruct(pattern.shape, jnp.int32)),
            operands[1], operands[2], space=pltpu.HBM,
            scratch=[
                pltpu.VMEM(factors.shape, bf16),
                pltpu.VMEM(pattern.shape, jnp.int32),
                pltpu.SemaphoreType.DMA((1 + pairs,)),
            ],
        )
        operands[2] = pattern_vmem
        value, out, right_sides, solver, *masked = call(
            first,
            (block_f32, spread_bf16, shaped(levels, rhs, width), jax.ShapeDtypeStruct((slots, deep, width), bf16))
            + tuple(jax.ShapeDtypeStruct((len(group), width, local_cols), bf16) for group in groups[1:]),
            *operands,
            spaces=[pltpu.HBM, pltpu.HBM, pltpu.VMEM, pltpu.HBM, pltpu.HBM],
            scratch=[
                pltpu.VMEM(factors.shape, bf16),
                pltpu.VMEM(inverses.shape, f32),
                pltpu.VMEM((1, levels), jnp.int32),
                pltpu.SemaphoreType.DMA((3 + pairs,)),
            ],
        )
        masked = [masked0, *masked]
    solved.append(value)
    blocks, moved = trade_beside(out, 0)
    gathered.append(blocks)
    held.append(moved)
    for level in range(1, levels - 1):
        with jax.named_scope("forward_level"):
            value, out = call(middle(level), (block_f32, spread_bf16), right_sides, solver, *gathered, *flat(held))
        solved.append(value)
        blocks, moved = trade_beside(out, level)
        gathered.append(blocks)
        if moved is not None:
            held.append(moved)
    factors = flat(held)
    results, rounded = {}, {}
    level = levels - 1
    with jax.named_scope("top_early"):
        arrived = factors[: len(factors) - (col_parts - 1)]
        early = call(top_early, block_f32, *gathered, *arrived)
    with jax.named_scope("top_level"):
        results[level], rounded[level], give = call(
            top, (block_f32, block_bf16, twins_f32), right_sides, solver, early, *gathered, *factors
        )

    def begin(lower):
        with jax.named_scope("backward_early"):
            known = [rounded[level] for level in range(lower + 2, levels)]
            return call(backward_early(lower), (twins_f32, twins_f32), *known, *factors)

    def keep_of(level, *begun):
        with jax.named_scope("backward_keep"):
            return call(keep_partials(level), twins_f32, rounded[level], *begun, *factors)

    keep = lambda: keep_of(levels - 1)
    for level in range(levels - 2, 0, -1):
        sums, begun = scatter(keep, give, lambda: begin(level - 1))
        with jax.named_scope("backward_level"):
            give, results[level], rounded[level] = call(
                down(level), (twins_f32, block_f32, block_bf16), solver, solved[level], sums, begun[1], *factors
            )
        keep = lambda level=level, begun=begun: keep_of(level, begun[0])
    sums, _ = scatter(keep, give)
    with jax.named_scope("backward_last"):
        return call(
            last,
            jax.ShapeDtypeStruct((levels, rhs, width), f32),
            solver,
            solved[0],
            sums,
            *[results[level] for level in range(1, levels)],
        )


def solution(mesh):
    parts = (mesh.shape["row"], mesh.shape["col"])

    def run(*operands):
        return local(parts, *operands)

    return jax.shard_map(
        run,
        mesh=mesh,
        in_specs=(
            P(None, "col", "row"),
            P(None, "row", "col"),
            P(None, "row", "col"),
            P(None, "row"),
            P(None, "row", None, None),
        ),
        out_specs=P(None, "col", "row"),
        check_vma=False,
    )
```

```python
import math

import jax
import jax.numpy as jnp
from jax import lax
from jax.experimental import pallas as pl
from jax.experimental.pallas import tpu as pltpu
from jax.sharding import PartitionSpec as P

HIGHEST = lax.Precision.HIGHEST


def pair_lookup(level_count):
    lookup = {}
    for lower_level in range(level_count):
        for above_level in range(lower_level + 1, level_count):
            lookup[above_level, lower_level] = len(lookup)
    return lookup


def call(kernel, outs, *operands, space=pltpu.VMEM, spaces=None, scratch=()):
    return pl.pallas_call(
        kernel,
        out_shape=outs,
        in_specs=[pl.BlockSpec(memory_space=s) for s in (spaces or [space] * len(operands))],
        out_specs=jax.tree.map(lambda _: pl.BlockSpec(memory_space=pltpu.VMEM), outs),
        scratch_shapes=scratch,
        compiler_params=pltpu.CompilerParams(vmem_limit_bytes=48 * 1024 * 1024),
    )(*operands)


def local(parts, right_sides, factors, pattern, live_widths, inverses):
    row_parts, col_parts = parts
    levels, rhs, width = right_sides.shape
    pairs, _, local_cols = factors.shape
    half = local_cols // width
    total_blocks = half * col_parts
    lookup = pair_lookup(levels)
    needed = [lookup[level, lower] for level in range(1, levels) for lower in range(level)]
    group_size = -(-pairs // (levels - 1))
    groups = [needed[k : k + group_size] for k in range(0, pairs, group_size)]
    place_of = {pair: (g, k) for g, group in enumerate(groups) for k, pair in enumerate(group)}
    inverses = inverses.reshape(levels, width, width)
    f32, bf16 = jnp.float32, jnp.bfloat16

    def shaped(*shape):
        return jax.ShapeDtypeStruct(shape, f32)

    block_f32 = jax.ShapeDtypeStruct((rhs, width), f32)
    block_bf16 = jax.ShapeDtypeStruct((rhs, width), bf16)
    spread_bf16 = jax.ShapeDtypeStruct((total_blocks, rhs, width), bf16)
    twins = row_parts // 2
    twins_f32 = jax.ShapeDtypeStruct((twins, rhs, width), f32)

    middle_row = 2 * (twins // 2 + 1) + 1
    row_order = [middle_row] + [k for k in range(0, row_parts, 2)] + [k for k in range(1, row_parts, 2) if k != middle_row]
    step = next(s for s in range(5, 5 + twins) if math.gcd(s, twins) == 1)
    twin_orders = [[(root + step * k) % twins for k in range(twins)] for root in (twins // 2, twins // 2 + 1)]

    def row_place(index):
        odd_place = twins + index // 2 + jnp.where(index < middle_row, 1, 0)
        odd_place = jnp.where(index == middle_row, 0, odd_place)
        return jnp.where(lax.rem(index, 2) == 0, 1 + index // 2, odd_place)

    def trade(blocks):
        return lax.all_to_all(blocks, "row", 0, 0, axis_index_groups=[row_order])

    def scatter(begin_keep, give, early=None):
        taken = lax.ppermute(give, "row", [(k, k ^ 1) for k in range(row_parts)])
        keep = begin_keep()
        begun = early() if early else ()
        with jax.named_scope("sum_twins"):
            sums = call(add, twins_f32, keep, taken)
        sums, begun = lax.optimization_barrier((sums, begun))
        one_of_each = [[2 * g + (g + side) % 2 for g in order] for side, order in zip((1, 0), twin_orders)]
        return lax.all_to_all(sums, "row", 0, 0, axis_index_groups=one_of_each), begun

    left_parts, right_parts = (0, 0, 1, 0, 1, 2), (0, 1, 0, 2, 1, 0)
    deep = len(left_parts) * width
    forward_slot = {level: level - 1 for level in range(1, levels - 1)}
    top_slot = levels - 2
    backward_slot = {level: levels - 1 + level for level in range(levels - 1)}
    slots = 2 * levels - 2

    def split(value):
        parts = []
        for _ in range(3):
            parts.append(value.astype(bf16))
            value = value - parts[-1].astype(f32)
        return parts

    def store_solver(solver_ref, slot, matrix):
        parts = split(matrix)
        for k, part in enumerate(right_parts):
            solver_ref[slot, k * width : (k + 1) * width, :] = parts[part]

    def solve(solver_ref, slot, vector):
        parts = split(vector)
        left = jnp.concatenate([parts[part] for part in left_parts], axis=1)
        return lax.dot_general(left, solver_ref[slot], (((1,), (0,)), ((), ())), preferred_element_type=f32)

    def forward_total(gathered, level, matrices, late=None, total=None):
        mine = lax.axis_index("col")
        for shift in range(col_parts):
            start = lax.rem(mine + shift, col_parts) * half
            for lower in range(level):
                is_late = shift > 0 and place_of[lookup[level, lower]][0] == level - 1
                if late is not None and is_late != late:
                    continue
                left = jnp.concatenate([gathered[lower][row_place(start + k)] for k in range(half)], axis=1)
                term = lax.dot_general(
                    left, matrix(matrices, level, lower, shift), (((1,), (1,)), ((), ())), preferred_element_type=f32
                )
                total = term if total is None else total + term
        return total

    def add(left_ref, right_ref, out_ref):
        index = lax.axis_index("row")
        second = lax.rem(index + index // 2, 2) == 0
        for place in range(twins):
            g = jnp.where(second, twin_orders[1][place], twin_orders[0][place])
            out_ref[place] = left_ref[g] + right_ref[g]

    def backward_partials(out_ref, solved, lower, matrices, begun, give):
        mine = lax.axis_index("col")
        index = lax.axis_index("row")
        for shift in range(col_parts):
            start = lax.rem(mine + shift, col_parts) * half
            pairs_of = [(start // 2 + k, 2 * k) for k in range(half // 2)]
            offsets = []
            for g, block in pairs_of:
                odd = lax.rem(index + index // 2 + g, 2)
                chosen = block + (1 - odd if give else odd)
                offsets.append(pl.multiple_of(chosen * width, width))
            total = None
            for level, vector in solved.items():
                group, place = place_of[lookup[level, lower]]
                ref = matrices[group * col_parts + shift]
                right = jnp.concatenate([ref[place, :, pl.ds(offset, width)] for offset in offsets], axis=1)
                term = lax.dot_general(vector, right, (((1,), (0,)), ((), ())), preferred_element_type=f32)
                total = term if total is None else total + term
            for k, (g, _) in enumerate(pairs_of):
                block = total[:, k * width : (k + 1) * width]
                out_ref[g] = block if begun is None else block + begun[g]

    def keep_partials(level):
        def body(rounded_ref, *refs):
            begun, matrices = (refs[0], refs[1:-1]) if level < levels - 1 else (None, refs[:-1])
            backward_partials(refs[-1], {level: rounded_ref[...]}, level - 1, matrices, begun, False)

        return body

    def spread(out_ref, value):
        out_ref[...] = jnp.broadcast_to(value.astype(bf16)[None], out_ref.shape)

    def mask_pair(out_ref, place, pattern_ref, factor_ref, pair):
        for block in range(half):
            columns = slice(block * width, (block + 1) * width)
            kept = jnp.broadcast_to(pattern_ref[pair][:, block : block + 1].astype(f32), (width, width))
            out_ref[place, :, columns] = factor_ref[pair, :, columns] * kept.astype(bf16)

    def first_mask(factor_hbm, pattern_hbm, masked_ref, pattern_out, factor_ref, pattern_ref, sems):
        order = groups[0]
        small = [pltpu.make_async_copy(pattern_hbm, pattern_ref, sems.at[0])]
        large = [
            pltpu.make_async_copy(factor_hbm.at[pair], factor_ref.at[pair], sems.at[1 + k])
            for k, pair in enumerate(order)
        ]
        for copy in small + large:
            copy.start()
        for copy in small:
            copy.wait()
        pattern_out[...] = pattern_ref[...]
        for copy, pair in zip(large, order):
            copy.wait()
            group, place = place_of[pair]
            mask_pair(masked_ref, place, pattern_ref, factor_ref, pair)

    def first(
        rhs_hbm, factor_hbm, pattern_ref, widths_hbm, inverse_hbm,
        solved_ref, out_ref, rhs_ref, solver_ref, *refs,
    ):
        masked_refs = [None, *refs[: len(groups) - 1]]
        factor_ref, inverse_ref, widths_ref, sems = refs[len(groups) - 1 :]
        later = needed[len(groups[0]) :]
        small = [
            pltpu.make_async_copy(widths_hbm, widths_ref, sems.at[0]),
            pltpu.make_async_copy(rhs_hbm, rhs_ref, sems.at[1]),
            pltpu.make_async_copy(inverse_hbm, inverse_ref, sems.at[2]),
        ]
        large = [
            pltpu.make_async_copy(factor_hbm.at[pair], factor_ref.at[pair], sems.at[3 + k])
            for k, pair in enumerate(later)
        ]
        for copy in small + large:
            copy.start()
        for copy in small:
            copy.wait()
        row = lax.broadcasted_iota(jnp.int32, (width, width), 0)
        column = lax.broadcasted_iota(jnp.int32, (width, width), 1)
        for level in range(levels):
            live = jnp.broadcast_to(widths_ref[:, level : level + 1], (width, width))
            inverse = jnp.where((row < live) & (column < live), inverse_ref[level], 0.0)
            if level == 0:
                value = lax.dot_general(
                    rhs_ref[0], inverse, (((1,), (1,)), ((), ())), precision=HIGHEST, preferred_element_type=f32
                )
                solved_ref[...] = value
                spread(out_ref, value)
            if level in forward_slot:
                store_solver(solver_ref, forward_slot[level], inverse.T)
            if level in backward_slot:
                store_solver(solver_ref, backward_slot[level], inverse)
            if level == levels - 1:
                both = lax.dot_general(
                    inverse, inverse, (((0,), (0,)), ((), ())), precision=HIGHEST, preferred_element_type=f32
                )
                store_solver(solver_ref, top_slot, both)
        for copy, pair in zip(large, later):
            copy.wait()
            group, place = place_of[pair]
            mask_pair(masked_refs[group], place, pattern_ref, factor_ref, pair)

    def flat(held):
        return [m for moved in held for m in moved]

    def matrix(refs, level, lower, shift):
        group, place = place_of[lookup[level, lower]]
        return refs[group * col_parts + shift][place]

    def middle(level):
        def body(rhs_ref, solver_ref, *refs):
            solved_ref, out_ref = refs[-2:]
            if level == 1:
                total = forward_total(refs[:1], level, refs[1:-2])
            else:
                gathered, matrices = refs[1 : 1 + level], refs[1 + level : -2]
                total = forward_total(gathered, level, matrices, True, refs[0][...])
            value = solve(solver_ref, forward_slot[level], rhs_ref[level] - total)
            solved_ref[...] = value
            spread(out_ref, value)

        return body

    def part_early(level):
        def body(*refs):
            refs[-1][...] = forward_total(refs[:level], level, refs[level:-1], False)

        return body

    def top_early(*refs):
        level = levels - 1
        refs[-1][...] = forward_total(refs[:level], level, refs[level:-1], False)

    def top(rhs_ref, solver_ref, early_ref, *refs):
        level = levels - 1
        gathered, matrices = refs[:level], refs[level:-3]
        result_ref, rounded_ref, give_ref = refs[-3:]
        total = forward_total(gathered, level, matrices, True, early_ref[...])
        result = solve(solver_ref, top_slot, rhs_ref[level] - total)
        result_ref[...] = result
        rounded = result.astype(bf16)
        rounded_ref[...] = rounded
        backward_partials(give_ref, {level: rounded}, level - 1, matrices, None, True)

    def backward_early(lower):
        known = range(lower + 2, levels)

        def body(*refs):
            solved = {level: refs[k][...] for k, level in enumerate(known)}
            matrices, (keep_ref, give_ref) = refs[len(known) : -2], refs[-2:]
            backward_partials(keep_ref, solved, lower, matrices, None, False)
            backward_partials(give_ref, solved, lower, matrices, None, True)

        return body

    def down(level):
        def body(solver_ref, solved_ref, sums_ref, early_give_ref, *refs):
            matrices = refs[:-3]
            give_ref, result_ref, rounded_ref = refs[-3:]
            corrected = solved_ref[...] - jnp.sum(sums_ref[...], axis=0)
            result = solve(solver_ref, backward_slot[level], corrected)
            result_ref[...] = result
            rounded = result.astype(bf16)
            rounded_ref[...] = rounded
            backward_partials(give_ref, {level: rounded}, level - 1, matrices, early_give_ref, True)

        return body

    def last(solver_ref, solved_ref, sums_ref, *refs):
        out_ref = refs[-1]
        corrected = solved_ref[...] - jnp.sum(sums_ref[...], axis=0)
        out_ref[0] = solve(solver_ref, backward_slot[0], corrected)
        for level in range(1, levels):
            out_ref[level] = refs[level - 1][...]

    def exchange(own):
        shifted = [own]
        for shift in range(1, col_parts):
            to_lower = [((q + shift) % col_parts, q) for q in range(col_parts)]
            shifted.append(lax.ppermute(own, "col", to_lower))
        return shifted

    def trade_beside(blocks, group):
        moved = exchange(masked[group]) if group < len(groups) else None
        blocks = trade(blocks)
        for later in range(group + 1, len(groups)):
            masked[later], blocks = lax.optimization_barrier((masked[later], blocks))
        return blocks, moved

    solved, gathered, held = [], [], []
    with jax.named_scope("forward_first"):
        operands = [
            pltpu.with_memory_space_constraint(x, pltpu.HBM)
            for x in (right_sides, factors, pattern, live_widths.reshape(1, levels), inverses)
        ]
        masked0, pattern_vmem = call(
            first_mask,
            (jax.ShapeDtypeStruct((len(groups[0]), width, local_cols), bf16), jax.ShapeDtypeStruct(pattern.shape, jnp.int32)),
            operands[1], operands[2], space=pltpu.HBM,
            scratch=[
                pltpu.VMEM(factors.shape, bf16),
                pltpu.VMEM(pattern.shape, jnp.int32),
                pltpu.SemaphoreType.DMA((1 + pairs,)),
            ],
        )
        operands[2] = pattern_vmem
        value, out, right_sides, solver, *masked = call(
            first,
            (block_f32, spread_bf16, shaped(levels, rhs, width), jax.ShapeDtypeStruct((slots, deep, width), bf16))
            + tuple(jax.ShapeDtypeStruct((len(group), width, local_cols), bf16) for group in groups[1:]),
            *operands,
            spaces=[pltpu.HBM, pltpu.HBM, pltpu.VMEM, pltpu.HBM, pltpu.HBM],
            scratch=[
                pltpu.VMEM(factors.shape, bf16),
                pltpu.VMEM(inverses.shape, f32),
                pltpu.VMEM((1, levels), jnp.int32),
                pltpu.SemaphoreType.DMA((3 + pairs,)),
            ],
        )
        masked = [masked0, *masked]
    solved.append(value)
    blocks, moved = trade_beside(out, 0)
    gathered.append(blocks)
    held.append(moved)
    for level in range(1, levels - 1):
        with jax.named_scope("forward_level"):
            early = []
            if level > 1:
                arrived = flat(held)[: -(col_parts - 1)]
                early = [call(part_early(level), block_f32, *gathered, *arrived)]
            value, out = call(
                middle(level), (block_f32, spread_bf16), right_sides, solver, *early, *gathered, *flat(held)
            )
        solved.append(value)
        blocks, moved = trade_beside(out, level)
        gathered.append(blocks)
        if moved is not None:
            held.append(moved)
    factors = flat(held)
    results, rounded = {}, {}
    level = levels - 1
    with jax.named_scope("top_early"):
        arrived = factors[: len(factors) - (col_parts - 1)]
        early = call(top_early, block_f32, *gathered, *arrived)
    with jax.named_scope("top_level"):
        results[level], rounded[level], give = call(
            top, (block_f32, block_bf16, twins_f32), right_sides, solver, early, *gathered, *factors
        )

    def begin(lower):
        with jax.named_scope("backward_early"):
            known = [rounded[level] for level in range(lower + 2, levels)]
            return call(backward_early(lower), (twins_f32, twins_f32), *known, *factors)

    def keep_of(level, *begun):
        with jax.named_scope("backward_keep"):
            return call(keep_partials(level), twins_f32, rounded[level], *begun, *factors)

    keep = lambda: keep_of(levels - 1)
    for level in range(levels - 2, 0, -1):
        sums, begun = scatter(keep, give, lambda: begin(level - 1))
        with jax.named_scope("backward_level"):
            give, results[level], rounded[level] = call(
                down(level), (twins_f32, block_f32, block_bf16), solver, solved[level], sums, begun[1], *factors
            )
        keep = lambda level=level, begun=begun: keep_of(level, begun[0])
    sums, _ = scatter(keep, give)
    with jax.named_scope("backward_last"):
        return call(
            last,
            jax.ShapeDtypeStruct((levels, rhs, width), f32),
            solver,
            solved[0],
            sums,
            *[results[level] for level in range(1, levels)],
        )


def solution(mesh):
    parts = (mesh.shape["row"], mesh.shape["col"])

    def run(*operands):
        return local(parts, *operands)

    return jax.shard_map(
        run,
        mesh=mesh,
        in_specs=(
            P(None, "col", "row"),
            P(None, "row", "col"),
            P(None, "row", "col"),
            P(None, "row"),
            P(None, "row", None, None),
        ),
        out_specs=P(None, "col", "row"),
        check_vma=False,
    )
```
